128 devices in a mesh: lat: 8 (over x, core), lon: 16 (over z, y).
Axes of the slice: x: 4, y: 4, z: 4, core: 2. Of those that a mesh axis runs over, the one named last changes fastest.
Arguments:
- noisy: bfloat16 [64, 128, 20480], P(None, 'lat', 'lon'), may hold values from -6 to 6
- coarse: bfloat16 [8, 64, 30, 128], P('lat', 'lon'), may hold values from -6 to 6
- owner: int32 [8, 16, 4, 4], P('lat', 'lon'), may hold values from 0 to 15, as said below
- local_slot: int32 [8, 16, 4, 4], P('lat', 'lon'), may hold values from 0 to 3
- weight_id: int32 [8, 16, 4, 4], P('lat', 'lon'), may hold values from 0 to 3
- counts: int32 [8, 16, 4], P('lat', 'lon'), may hold values from 1 to 4, 12 in all within a row
- interp_table: bfloat16 [4, 128, 5120], replicated, may hold values from -0.3125 to 0.3125
- conv_in: bfloat16 [3, 3, 64, 64], replicated, may hold values from -0.25 to 0.25
- conv_cond: bfloat16 [3, 3, 64, 30], replicated, may hold values from -0.375 to 0.375
- bias_in: float32 [64], replicated, may hold values from -4 to 4
- conv_out: bfloat16 [3, 3, 64, 64], replicated, may hold values from -0.25 to 0.25
- bias_out: float32 [64], replicated, may hold values from -4 to 4
Outputs:
- updated: bfloat16 [64, 128, 20480], P(None, 'lat', 'lon')
The draws below stay inside these ranges and needn't reach their ends.
Inputs may be any that keep to these rules, and one draw needn't show every extreme that they name: `owner`: in the lists of one device (its 4 x 4 slots, live or not) no lon index is named by more than 6 slots, and some is named by exactly 6. The 4 counts of one device sum to 12, and the largest is 4.
All inputs are finite; a program needn't handle non-finite values.
Results may differ from the reference program's by a relative error of at most 0.0041.
Values may be sent and summed in bfloat16 or wider, within the bound.
No kernel may reach another device: no remote copies, remote signals or barrier semaphores. Data moves between devices by JAX's collectives and lax.ppermute only.
A program may use at most 256 MiB of HBM per device.

```python
import math
import jax
import jax.numpy as jnp
import numpy as np
from jax import lax

C = 64
CC = 30
FR = 16
FC = 1280
BC = 128
CBD = 4
SUB = 4
KMAX = 4
CAP = 6
LIVE = 12
NW = 4
SR = 4
FB = 5120
ROWS = 128
COLS = 20480
LATG = 8
LONG = 16
LONBLK = 64


def draw_owner(key, part):
    key = jax.random.fold_in(key, 11)
    total = SUB * KMAX

    def one_device(sub_key):
        key_a, key_b, key_c = jax.random.split(sub_key, 3)
        heavy = jax.random.randint(key_a, (), 0, LONG)
        start = jax.random.randint(key_b, (), 0, LONG - 1)
        places = jnp.arange(total, dtype=jnp.int32)
        rest = (heavy + 1 + (start + places - CAP) % (LONG - 1)) % LONG
        named = jnp.where(places < CAP, heavy, rest)
        order = jax.random.permutation(key_c, total)
        return named[order].reshape(SUB, KMAX)
    keys = jax.random.split(key, LATG * LONG)
    drawn = jax.vmap(one_device)(keys)
    return drawn.reshape(LATG, LONG, SUB, KMAX).astype(jnp.int32)


def place_ends(values, stream_key, least, top_value):
    dims = values.shape
    place = [jax.random.randint(jax.random.fold_in(stream_key, axis), (), 0, dims[axis]) for axis in range(len(dims))]
    values = values.at[tuple(place)].set(least)
    longest = dims.index(max(dims))
    place[longest] = (place[longest] + 1) % dims[longest]
    return values.at[tuple(place)].set(top_value)


def block_levels(stream_key, extent, cuts, smallest, largest):
    level = 1.0
    for dim, blocks in cuts:
        steps = jax.random.uniform(jax.random.fold_in(jax.random.fold_in(stream_key, 6), dim), (blocks,), jnp.float32, smallest / len(cuts), largest / len(cuts))
        level = level * jnp.repeat(jnp.exp(steps), extent[dim] // blocks).reshape((-1,) + (1,) * (len(extent) - 1 - dim))
    return level


def split_up(number_of, total, most, slope):
    weights = [(1 << 20) // math.isqrt(standing ** slope) + 1 for standing in range(2, number_of + 1)]
    spare, given = total - most - (number_of - 1), [1] * (number_of - 1)
    while spare > 0:
        movable = [i for i in range(number_of - 1) if given[i] < most]
        whole, left = sum([weights[i] for i in movable]), spare
        for i in movable:
            more = min(most - given[i], max(1, left * weights[i] // whole), spare)
            given[i] = given[i] + more
            spare = spare - more
    return np.array([most] + given)


def ragged_sizes(own_key, count, total, reach, lean):
    if count == 2:
        one = jax.random.randint(own_key, (), max(1, total - reach), min(reach, total - 1) + 1)
        return jnp.stack([one, total - one])
    lengths = jnp.asarray(split_up(count, total, reach, lean), jnp.int32)
    couples = (count - 1) // 2
    giver, receiver = lengths[1:1 + 2 * couples:2], lengths[2:2 + 2 * couples:2]
    slack = jnp.minimum(giver - 1, reach - receiver)
    moved = jax.random.randint(jax.random.fold_in(own_key, 1), (couples,), 0, 1 << 20) % (slack + 1)
    lengths = lengths.at[1:1 + 2 * couples:2].set(giver - moved).at[2:2 + 2 * couples:2].set(receiver + moved)
    return lengths[jax.random.permutation(jax.random.fold_in(own_key, 2), count)]


def gaussian(own_key, shape, spread, bound, cuts=(), kind=jnp.bfloat16):
    array = jax.random.normal(own_key, shape, jnp.float32) * spread
    if len(cuts) > 0:
        array = block_levels(own_key, shape, cuts, -0.22, 0.18) * array
    return jnp.clip(array, min=-bound, max=bound).astype(kind)


def setup_inputs(seed: int = 0) -> dict:
    seeds = jax.random.split(jax.random.key(seed), 13)
    return {
        "noisy": gaussian(seeds[0], (C, ROWS, COLS), 1.0, 6.0, ((1, 8), (2, 16))),
        "coarse": gaussian(seeds[1], (LATG, LONBLK, CC, BC), 1.0, 6.0, ((0, 8), (1, 16))),
        "owner": draw_owner(jax.random.fold_in(seeds[12], 71), 0),
        "local_slot": place_ends(jax.random.randint(seeds[3], (LATG, LONG, SUB, KMAX), 0, CBD), jax.random.fold_in(seeds[3], 1), 0, CBD - 1).astype(jnp.int32),
        "weight_id": place_ends(jax.random.randint(seeds[4], (LATG, LONG, SUB, KMAX), 0, NW), jax.random.fold_in(seeds[4], 1), 0, NW - 1).astype(jnp.int32),
        "counts": jax.vmap(lambda own: ragged_sizes(own, SUB, LIVE, KMAX, 0))(jax.random.split(seeds[5], LATG * LONG)).reshape((LATG, LONG, SUB)).astype(jnp.int32),
        "interp_table": gaussian(seeds[6], (NW, BC, FB), (BC * 3) ** -0.5, 0.3125),
        "conv_in": gaussian(seeds[7], (3, 3, C, C), (9 * C) ** -0.5, 0.25),
        "conv_cond": gaussian(seeds[8], (3, 3, C, CC), (9 * CC) ** -0.5, 0.375),
        "bias_in": gaussian(seeds[9], (C,), 0.7, 4.0, (), jnp.float32),
        "conv_out": gaussian(seeds[10], (3, 3, C, C), (9 * C) ** -0.5, 0.25),
        "bias_out": gaussian(seeds[11], (C,), 0.7, 4.0, (), jnp.float32),
    }


def interpolate(blocks, ids, interp_table):
    table = interp_table.astype(jnp.float32).reshape(NW * BC, FB)

    def one_tile(pair):
        blk, idx = pair
        onehot = (idx[:, None] == jnp.arange(NW, dtype=jnp.int32)[None, :]).astype(jnp.float32)
        grouped = jnp.einsum("kw,kcb->cwb", onehot, blk.astype(jnp.float32)).astype(jnp.bfloat16)
        grouped = lax.optimization_barrier(grouped).astype(jnp.float32).reshape(CC, NW * BC)
        return jnp.dot(grouped, table, preferred_element_type=jnp.float32)
    return lax.map(one_tile, (blocks, ids))


def conv_rows(padded, kernel):
    rows = padded.shape[1] - 2
    cols = padded.shape[2] - 2
    total = jnp.zeros((kernel.shape[2], rows, cols), jnp.float32)
    for shift_r in range(3):
        for shift_c in range(3):
            window = padded[:, shift_r:shift_r + rows, shift_c:shift_c + cols]
            total = total + jnp.einsum("oc,crw->orw", kernel[shift_r, shift_c].astype(jnp.float32), window.astype(jnp.float32))
    return total


def pad_field(field):
    wrapped = jnp.concatenate([field[:, :, -1:], field, field[:, :, :1]], axis=2)
    return jnp.pad(wrapped, ((0, 0), (1, 1), (0, 0)))


def blockwise_conv(padded, kernel):
    def one_band(band):
        start = (band * FR).astype(jnp.int32)
        piece = lax.dynamic_slice_in_dim(padded, start, FR + 2, 1)
        return conv_rows(piece, kernel)
    bands = lax.map(one_band, jnp.arange(LATG, dtype=jnp.int32))
    return jnp.transpose(bands, (1, 0, 2, 3)).reshape(kernel.shape[2], ROWS, COLS)


def reference(noisy, coarse, owner, local_slot, weight_id, counts, interp_table, conv_in, conv_cond, bias_in, conv_out, bias_out):
    lat_index = jnp.arange(LATG, dtype=jnp.int32)[:, None, None, None]
    blocks = coarse[lat_index, owner * CBD + local_slot]
    live = jnp.arange(KMAX, dtype=jnp.int32)[None, None, None, :] < counts[..., None]
    blocks = jnp.where(live[..., None, None], blocks, jnp.zeros_like(blocks))
    flat_blocks = blocks.reshape(LATG * LONG * SUB, KMAX, CC, BC)
    flat_ids = weight_id.reshape(LATG * LONG * SUB, KMAX)
    tiles = interpolate(flat_blocks, flat_ids, interp_table).astype(jnp.bfloat16)
    cond = tiles.reshape(LATG, LONG, SUB, CC, SR, FC)
    cond = jnp.transpose(cond, (3, 0, 2, 4, 1, 5)).reshape(CC, ROWS, COLS)
    hidden = blockwise_conv(pad_field(noisy), conv_in) + blockwise_conv(pad_field(cond), conv_cond)
    hidden = hidden + bias_in[:, None, None]
    act = jax.nn.silu(hidden).astype(jnp.bfloat16)
    result = noisy.astype(jnp.float32) + blockwise_conv(pad_field(act), conv_out) + bias_out[:, None, None]
    return result.astype(jnp.bfloat16)
```

```python
import jax
import jax.numpy as jnp
from jax import lax
from jax.experimental import pallas as pl
from jax.experimental.pallas import tpu as pltpu
from jax.sharding import PartitionSpec as P

BF = jnp.bfloat16
F32 = jnp.float32
MIB = 1024 * 1024

C = 64
CP = 32
R = 16
W = 1280
LT = 128
WX = W + LT
PEERS = 16
HELD = 4
SUBS = 4
SLOTS = 4
KINDS = 4
MSG = HELD * CP + C


def vmem(n=1):
    return [pl.BlockSpec(memory_space=pltpu.VMEM)] * n


def smem(n=1):
    return [pl.BlockSpec(memory_space=pltpu.SMEM)] * n


def params(mib):
    return pltpu.CompilerParams(vmem_limit_bytes=mib * MIB)


def struct(shape, dtype=BF):
    return jax.ShapeDtypeStruct(shape, dtype)


def iota(shape, dim):
    return lax.broadcasted_iota(jnp.int32, shape, dim)


def message_kernel(first, last, coarse, owner, slot, weight, counts, out):
    lane = iota((C, R, LT), 2)
    edge = jnp.where(lane < 64, first[...].astype(F32), last[...].astype(F32))
    edge = jnp.swapaxes(edge.astype(BF), 0, 1)
    edge = jnp.concatenate([edge[r] for r in range(R)], axis=1)
    row = iota((R * LT, LT), 0)
    col = iota((R * LT, LT), 1)
    at = row % LT
    kind = jnp.where(at < 64, at, at - 124)
    wanted = ((at < 2) | (at >= 126)) & (col == kind * R + row // LT)
    pick = jnp.where(wanted, 1.0, 0.0).astype(BF)
    packed = jnp.dot(edge, pick, preferred_element_type=F32)
    lanes = iota((C, LT), 1)
    for s in range(SUBS):
        live = counts[0, 0, s]
        for k in range(SLOTS):
            n = s * SLOTS + k
            block = owner[0, 0, s, k] * HELD + slot[0, 0, s, k]
            kind_id = jnp.where(k < live, weight[0, 0, s, k], KINDS)
            packed = jnp.where(lanes == 64 + n, block.astype(F32), packed)
            packed = jnp.where(lanes == 80 + n, kind_id.astype(F32), packed)
    packed = packed.astype(BF)
    zeros = jnp.zeros((CP - coarse.shape[2], LT), F32)
    blocks = [jnp.concatenate([coarse[0, b].astype(F32), zeros], axis=0).astype(BF) for b in range(HELD)]
    whole = jnp.concatenate(blocks + [packed], axis=0)
    for p in range(PEERS):
        out[p] = whole


def message(noisy, coarse, owner, slot, weight, counts):
    return pl.pallas_call(
        message_kernel,
        grid=(1,),
        out_shape=struct((PEERS, MSG, LT)),
        in_specs=[
            pl.BlockSpec((C, R, LT), lambda i: (0, 0, 0)),
            pl.BlockSpec((C, R, LT), lambda i: (0, 0, W // LT - 1)),
            pl.BlockSpec(coarse.shape, lambda i: (0, 0, 0, 0)),
        ]
        + smem(4),
        out_specs=pl.BlockSpec((PEERS, MSG, LT), lambda i: (0, 0, 0)),
        compiler_params=params(12),
    )(noisy, noisy, coarse, owner, slot, weight, counts)


def shifted(x, width):
    return [pltpu.roll(x, 1, 1), x, pltpu.roll(x, width - 1, 1)]


def pair_weights(kernel, pad):
    out_ch = kernel.shape[2]
    def block(dr, dc):
        w = kernel[dr, dc]
        if pad:
            w = jnp.concatenate([w.astype(F32), jnp.zeros((out_ch, pad), F32)], axis=1).astype(BF)
        return w
    rows = jnp.concatenate([block(dr, dc) for dr in range(3) for dc in range(3)], axis=1)
    blank = jnp.zeros((out_ch, rows.shape[1] // 3), BF)
    return jnp.concatenate(
        [jnp.concatenate([rows, blank], axis=1), jnp.concatenate([blank, rows], axis=1)], axis=0
    )


def own_kernel(noisy, conv_in, conv_cond, conv_out, xs, hid, w_in, w_cond, w_out, x3):
    w_in[...] = pair_weights(conv_in, 0)
    w_out[...] = pair_weights(conv_out, 0)
    w_cond[...] = pair_weights(conv_cond, CP - conv_cond.shape[3])
    xs[...] = jnp.swapaxes(noisy[...], 0, 1).reshape(R * C, W)
    blank = jnp.zeros((C, LT), BF)
    for r in range(R):
        x = jnp.concatenate([xs[pl.ds(r * C, C), :], blank], axis=1)
        for d, y in enumerate(shifted(x, WX)):
            x3[pl.ds((r * 3 + d) * C, C), :] = y
    for i in range(R // 2 - 1):
        hid[pl.ds(i * 2 * C, 2 * C), :] = jnp.dot(
            w_in[...], x3[pl.ds(i * 6 * C, 12 * C), :], preferred_element_type=F32
        )


def own_tile(noisy, conv_in, conv_cond, conv_out):
    return pl.pallas_call(
        own_kernel,
        out_shape=(
            struct((R * C, W)),
            struct(((R - 2) * C, WX), F32),
            struct((2 * C, 12 * C)),
            struct((2 * C, 12 * CP)),
            struct((2 * C, 12 * C)),
        ),
        in_specs=vmem(4),
        out_specs=tuple(vmem(5)),
        scratch_shapes=[pltpu.VMEM((R * 3 * C, WX), BF)],
        compiler_params=params(28),
        cost_estimate=pl.CostEstimate(flops=3 * 10**9, bytes_accessed=12 * 10**6, transcendentals=0),
    )(noisy, conv_in, conv_cond, conv_out)


def cond_kernel(got, owner, slot, weight, counts, table, xs, cond, halo, top, bottom, acc, grp, ints, lists, sem):
    me = lax.axis_index("lon")
    left = lax.rem(me + PEERS - 1, PEERS)
    right = lax.rem(me + 1, PEERS)
    edge_l = got[left, pl.ds(HELD * CP, C), :]
    edge_r = got[right, pl.ds(HELD * CP, C), :]
    ints[0] = edge_l[0:8].astype(F32).astype(jnp.int32)
    ints[1] = edge_r[0:8].astype(F32).astype(jnp.int32)
    copy = pltpu.make_async_copy(ints, lists, sem)
    copy.start()
    acc[...] = jnp.zeros_like(acc)

    def add(d, s, block, kind):
        part = got[block // HELD, pl.ds(pl.multiple_of(lax.rem(block, HELD) * CP, CP), CP), :]
        at = (d * SUBS + s) * (KINDS + 1) + kind
        acc[at] = acc[at] + part.astype(F32)

    for s in range(SUBS):
        for k in range(SLOTS):
            kind = jnp.where(k < counts[0, 0, s], weight[0, 0, s, k], KINDS)
            add(0, s, owner[0, 0, s, k] * HELD + slot[0, 0, s, k], kind)

    lane = iota((C, LT), 1)
    both = jnp.where(lane < 32, edge_r.astype(F32), jnp.where(lane < 64, edge_l.astype(F32), 0.0)).astype(BF)
    src = iota((LT, R * LT), 0)
    dst = iota((LT, R * LT), 1)
    at = dst % LT
    kind = jnp.where(at < 64, at, at - 124)
    wanted = ((at < 2) | (at >= 126)) & (src == kind * R + dst // LT)
    place = jnp.where(wanted, 1.0, 0.0).astype(BF)
    tiles = jnp.dot(both, place, preferred_element_type=F32).astype(BF)
    for r in range(R):
        halo[pl.ds(r * C, C), :] = tiles[:, r * LT : (r + 1) * LT]

    copy.wait()
    for d in range(2):
        for s in range(SUBS):
            for k in range(SLOTS):
                n = s * SLOTS + k
                add(d + 1, s, lists[d, 0, 64 + n], lists[d, 0, 80 + n])
    for d in range(3):
        for s in range(SUBS):
            for w in range(KINDS):
                grp[d, pl.ds(s * CP, CP), w * LT : (w + 1) * LT] = acc[(d * SUBS + s) * (KINDS + 1) + w].astype(BF)

    lane = iota((SUBS * CP, LT), 1)
    for r in range(R // SUBS):
        own = jnp.dot(grp[0], table[:, r * W : (r + 1) * W], preferred_element_type=F32).astype(BF)
        lhs = jnp.dot(grp[1], table[:, (r + 1) * W - LT : (r + 1) * W], preferred_element_type=F32)
        rhs = jnp.dot(grp[2], table[:, r * W : r * W + LT], preferred_element_type=F32)
        side = jnp.where(lane < 2, rhs, jnp.where(lane >= 126, lhs, 0.0)).astype(BF)
        for s in range(SUBS):
            at = pl.ds((s * SUBS + r) * CP, CP)
            cond[at, 0:W] = own[s * CP : (s + 1) * CP]
            cond[at, W:WX] = side[s * CP : (s + 1) * CP]
    for out, r0 in ((top, 0), (bottom, R - 2)):
        out[0 : 2 * C, 0:W] = xs[pl.ds(r0 * C, 2 * C), :]
        out[0 : 2 * C, W:WX] = halo[pl.ds(r0 * C, 2 * C), :]
        out[2 * C : 2 * C + 2 * CP, :] = cond[pl.ds(r0 * CP, 2 * CP), :]


def cond_tile(got, owner, slot, weight, counts, table, xs):
    edge = struct((2 * (C + CP), WX))
    return pl.pallas_call(
        cond_kernel,
        out_shape=(struct((R * CP, WX)), struct((R * C, LT)), edge, edge),
        in_specs=vmem(1) + smem(4) + vmem(2),
        out_specs=tuple(vmem(4)),
        scratch_shapes=[
            pltpu.VMEM((3 * SUBS * (KINDS + 1), CP, LT), F32),
            pltpu.VMEM((3, SUBS * CP, KINDS * LT), BF),
            pltpu.VMEM((2, 8, LT), jnp.int32),
            pltpu.SMEM((2, 8, LT), jnp.int32),
            pltpu.SemaphoreType.DMA,
        ],
        compiler_params=params(20),
    )(got, owner, slot, weight, counts, table, xs)


def silu(v):
    return v / (1.0 + jnp.exp(-v))


def inner_kernel(hid, cond, halo, w_in, w_cond, bias, act, c3, h3):
    for r in range(R):
        for d, y in enumerate(shifted(cond[pl.ds(r * CP, CP), :], WX)):
            c3[pl.ds((r * 3 + d) * CP, CP), :] = y
        blank = jnp.zeros((C, LT), BF)
        h = jnp.concatenate([blank, halo[pl.ds(r * C, C), :], blank], axis=1)
        for d, y in enumerate(shifted(h, 3 * LT)):
            h3[pl.ds((r * 3 + d) * C, C), :] = y
    for i in range(R // 2 - 1):
        at = pl.ds(i * 2 * C, 2 * C)
        v = jnp.dot(w_cond[...], c3[pl.ds(i * 6 * CP, 12 * CP), :], preferred_element_type=F32)
        v = v + hid[at, :] + bias[...]
        e = jnp.dot(w_in[...], h3[pl.ds(i * 6 * C, 12 * C), :], preferred_element_type=F32)
        act[at, LT : W - LT] = silu(v[:, LT : W - LT]).astype(BF)
        act[at, W - LT : WX] = silu(v[:, W - LT : WX] + e[:, 0 : 2 * LT]).astype(BF)
        act[at, 0:LT] = silu(v[:, 0:LT] + e[:, 2 * LT : 3 * LT]).astype(BF)


def inner_rows(hid, cond, halo, w_in, w_cond, bias):
    return pl.pallas_call(
        inner_kernel,
        out_shape=struct(((R - 2) * C, WX)),
        in_specs=vmem(6),
        out_specs=vmem()[0],
        scratch_shapes=[
            pltpu.VMEM((R * 3 * CP, WX), BF),
            pltpu.VMEM((R * 3 * C, 3 * LT), BF),
        ],
        compiler_params=params(24),
        cost_estimate=pl.CostEstimate(flops=2 * 10**9, bytes_accessed=10 * 10**6, transcendentals=10**6),
    )(hid, cond, halo, w_in, w_cond, bias)


def outer_kernel(act, top, bottom, above, below, xs, w_in, w_cond, w_out, bias, bias_out, out, n3, c3, a3, z):
    lat = lax.axis_index("lat")
    first = jnp.where(lat == 0, 0.0, 1.0)
    last = jnp.where(lat == 7, 0.0, 1.0)

    def put(row, x):
        for d, y in enumerate(shifted(x, WX)):
            a3[pl.ds((row * 3 + d) * C, C), :] = y[:, 0:W]

    for r in range(R - 2):
        put(r + 2, act[pl.ds(r * C, C), :])
    for part, (lo, hi) in enumerate(((above, top), (bottom, below))):
        for r, ref in enumerate((lo, lo, hi, hi)):
            for d, y in enumerate(shifted(ref[pl.ds(r % 2 * C, C), :], WX)):
                n3[pl.ds((r * 3 + d) * C, C), :] = y
            for d, y in enumerate(shifted(ref[pl.ds(2 * C + r % 2 * CP, CP), :], WX)):
                c3[pl.ds((r * 3 + d) * CP, CP), :] = y
        v = jnp.dot(w_in[...], n3[...], preferred_element_type=F32)
        v = v + jnp.dot(w_cond[...], c3[...], preferred_element_type=F32) + bias[...]
        v = silu(v)
        if part == 0:
            put(0, (v[0:C] * first).astype(BF))
            put(1, v[C:].astype(BF))
        else:
            put(R, v[0:C].astype(BF))
            put(R + 1, (v[C:] * last).astype(BF))
    for i in range(R // 2):
        at = pl.ds(i * 2 * C, 2 * C)
        y = jnp.dot(w_out[...], a3[pl.ds(i * 6 * C, 12 * C), :], preferred_element_type=F32)
        z[at, :] = (y + xs[at, :].astype(F32) + bias_out[...]).astype(BF)
    out[...] = jnp.swapaxes(z[...].reshape(R, C, W), 0, 1)


def outer_rows(act, top, bottom, above, below, xs, w_in, w_cond, w_out, bias, bias_out):
    return pl.pallas_call(
        outer_kernel,
        out_shape=struct((C, R, W)),
        in_specs=vmem(11),
        out_specs=vmem()[0],
        scratch_shapes=[
            pltpu.VMEM((12 * C, WX), BF),
            pltpu.VMEM((12 * CP, WX), BF),
            pltpu.VMEM(((R + 2) * 3 * C, W), BF),
            pltpu.VMEM((R * C, W), BF),
        ],
        compiler_params=params(32),
    )(act, top, bottom, above, below, xs, w_in, w_cond, w_out, bias, bias_out)


def local(noisy, coarse, owner, slot, weight, counts, table, conv_in, conv_cond, bias_in, conv_out, bias_out):
    msg = message(noisy, coarse, owner, slot, weight, counts)
    got = lax.all_to_all(msg, "lon", split_axis=0, concat_axis=0, tiled=True)
    xs, hid, w_in, w_cond, w_out = own_tile(noisy, conv_in, conv_cond, conv_out)
    table = table.reshape(KINDS * LT, table.shape[2])
    cond, halo, top, bottom = cond_tile(got, owner, slot, weight, counts, table, xs)
    count = lax.axis_size("lat")
    above = lax.ppermute(bottom, "lat", [(i, i + 1) for i in range(count - 1)])
    below = lax.ppermute(top, "lat", [(i + 1, i) for i in range(count - 1)])
    bias = jnp.concatenate([bias_in, bias_in])[:, None]
    bias_2 = jnp.concatenate([bias_out, bias_out])[:, None]
    act = inner_rows(hid, cond, halo, w_in, w_cond, bias)
    return outer_rows(act, top, bottom, above, below, xs, w_in, w_cond, w_out, bias, bias_2)


def solution(mesh):
    grid = P("lat", "lon")
    in_specs = (P(None, "lat", "lon"),) + (grid,) * 5 + (P(),) * 6
    return jax.shard_map(local, mesh=mesh, in_specs=in_specs, out_specs=P(None, "lat", "lon"), check_vma=False)
```

```python
import jax
import jax.numpy as jnp
from jax import lax
from jax.experimental import pallas as pl
from jax.experimental.pallas import tpu as pltpu
from jax.sharding import PartitionSpec as P

BF = jnp.bfloat16
F32 = jnp.float32
MIB = 1024 * 1024

C = 64
CP = 32
R = 16
W = 1280
LT = 128
WX = W + LT
PEERS = 16
HELD = 4
SUBS = 4
SLOTS = 4
KINDS = 4
EDGE = 16
MSG = HELD * CP + EDGE
PAIRS = R // 2 - 1
TAPS = 12 * C
TAPS_C = 12 * CP
PARTS = 4


def vmem(n=1):
    return [pl.BlockSpec(memory_space=pltpu.VMEM)] * n


def smem(n=1):
    return [pl.BlockSpec(memory_space=pltpu.SMEM)] * n


def params(mib):
    return pltpu.CompilerParams(vmem_limit_bytes=mib * MIB)


def struct(shape, dtype=BF):
    return jax.ShapeDtypeStruct(shape, dtype)


def kept(shape, dtype=BF):
    return pltpu.VMEM(shape, dtype)


def hbm(n=1):
    return [pl.BlockSpec(memory_space=pltpu.HBM)] * n


def in_hbm(*arrays):
    return [pltpu.with_memory_space_constraint(a, pltpu.HBM) for a in arrays]


def in_vmem(*arrays):
    return [pltpu.with_memory_space_constraint(a, pltpu.VMEM) for a in arrays]


def iota(shape, dim):
    return lax.broadcasted_iota(jnp.int32, shape, dim)


def message_kernel(first, last, coarse, owner, slot, weight, counts, out):
    me = lax.axis_index("lon")
    lane = iota((C, R, LT), 2)
    edge = jnp.where(lane < 64, first[...].astype(F32), last[...].astype(F32))
    edge = jnp.swapaxes(edge.astype(BF), 0, 1)
    edge = jnp.concatenate([edge[r] for r in range(R)], axis=1)
    row = iota((R * LT, LT), 0)
    col = iota((R * LT, LT), 1)
    at = row % LT
    kind = jnp.where(at < 64, at, at - 124)
    wanted = ((at < 2) | (at >= 126)) & (col == kind * R + row // LT)
    pick = jnp.where(wanted, 1.0, 0.0).astype(BF)
    packed = jnp.dot(edge, pick, preferred_element_type=F32)
    sides = []
    for side in range(2):
        parts = [packed[g * EDGE : (g + 1) * EDGE, side * 32 : side * 32 + 32] for g in range(C // EDGE)]
        sides.append(jnp.concatenate(parts, axis=1))
    lanes = iota((2, HELD, LT), 2)
    lists = jnp.zeros((2, HELD, LT), F32)
    for s in range(SUBS):
        live = counts[0, 0, s]
        for k in range(SLOTS):
            n = s * SLOTS + k
            block = owner[0, 0, s, k] * HELD + slot[0, 0, s, k]
            kind_id = jnp.where(k < live, weight[0, 0, s, k], KINDS)
            lists = jnp.where(lanes == n, block.astype(F32), lists)
            lists = jnp.where(lanes == 16 + n, kind_id.astype(F32), lists)
    chans = coarse[0].astype(F32)
    blocks = jnp.swapaxes(jnp.concatenate([chans, lists], axis=0), 0, 1)
    blocks = blocks.reshape(HELD * CP, LT).astype(BF)
    right = lax.rem(me + 1, PEERS)
    for p in range(PEERS):
        out[p, 0 : HELD * CP] = blocks
        out[p, HELD * CP :] = jnp.where(right == p, sides[1], sides[0]).astype(BF)


def message(noisy, coarse, owner, slot, weight, counts):
    return pl.pallas_call(
        message_kernel,
        grid=(1,),
        out_shape=struct((PEERS, MSG, LT)),
        in_specs=[
            pl.BlockSpec((C, R, LT), lambda i: (0, 0, 0)),
            pl.BlockSpec((C, R, LT), lambda i: (0, 0, W // LT - 1)),
            pl.BlockSpec(coarse.shape, lambda i: (0, 0, 0, 0)),
        ]
        + smem(4),
        out_specs=pl.BlockSpec((PEERS, MSG, LT), lambda i: (0, 0, 0)),
        compiler_params=params(12),
    )(*in_hbm(noisy, noisy, coarse, owner, slot, weight, counts))


def load(src, dst, sem):
    copy = pltpu.make_async_copy(src, dst, sem)
    copy.start()
    return copy


def shifted(x, width):
    return [pltpu.roll(x, 1, 1), x, pltpu.roll(x, width - 1, 1)]


def pair_weights(taps):
    rows = jnp.concatenate(taps, axis=1)
    blank = jnp.zeros((rows.shape[0], rows.shape[1] // 3), BF)
    return jnp.concatenate(
        [jnp.concatenate([rows, blank], axis=1), jnp.concatenate([blank, rows], axis=1)], axis=0
    )


def cond_tap(tap):
    tap = jnp.concatenate([tap.astype(F32), jnp.zeros((CP - tap.shape[0], tap.shape[1]), F32)], axis=0)
    return tap.T.astype(BF)


def bias_column(row):
    same = iota((C, C), 0) == iota((C, C), 1)
    column = jnp.sum(jnp.where(same, row, 0.0), axis=1, keepdims=True)
    return jnp.concatenate([column, column], axis=0)


def own_kernel(noisy, conv_in, conv_cond, conv_out, bias_in, bias_out, xs, hid, wts, bias, x3, buf, sems):
    loads = []
    for g in range(PARTS):
        part = pl.ds(g * (C // PARTS), C // PARTS)
        loads.append(load(noisy.at[part], buf.at[part], sems.at[g]))
    taps = [(i, j) for i in range(3) for j in range(3)]
    wts[:, 0:TAPS] = pair_weights([conv_in[i, j] for i, j in taps])
    wts[:, TAPS : 2 * TAPS] = pair_weights([conv_out[i, j] for i, j in taps])
    wts[:, 2 * TAPS :] = pair_weights([cond_tap(conv_cond[i, j]) for i, j in taps])
    bias[:, 0:LT] = jnp.broadcast_to(bias_column(bias_in[...]), (2 * C, LT))
    bias[:, LT:] = jnp.broadcast_to(bias_column(bias_out[...]), (2 * C, LT))
    for copy in loads:
        copy.wait()
    xs[...] = jnp.swapaxes(buf[...], 0, 1).reshape(R * C, W)
    blank = jnp.zeros((C, LT), BF)
    for r in range(R):
        x = jnp.concatenate([xs[pl.ds(r * C, C), :], blank], axis=1)
        for d, y in enumerate(shifted(x, WX)):
            x3[pl.ds((r * 3 + d) * C, C), :] = y
    for i in range(PAIRS):
        v = jnp.dot(wts[:, 0:TAPS], x3[pl.ds(i * 6 * C, 12 * C), :], preferred_element_type=F32)
        hid[i] = (v + bias[:, 0:1]).astype(BF)


def own_tile(noisy, conv_in, conv_cond, conv_out, bias_in, bias_out):
    return pl.pallas_call(
        own_kernel,
        out_shape=(
            kept((R * C, W)),
            kept((PAIRS, 2 * C, WX)),
            kept((2 * C, 2 * TAPS + TAPS_C)),
            kept((2 * C, 2 * LT), F32),
        ),
        in_specs=hbm(1) + vmem(5),
        out_specs=tuple(vmem(4)),
        scratch_shapes=[
            pltpu.VMEM((R * 3 * C, WX), BF),
            pltpu.VMEM((C, R, W), BF),
            pltpu.SemaphoreType.DMA((PARTS,)),
        ],
        compiler_params=params(18),
        cost_estimate=pl.CostEstimate(flops=3 * 10**9, bytes_accessed=12 * 10**6, transcendentals=0),
    )(*in_hbm(noisy, conv_in, conv_cond, conv_out, bias_in, bias_out))


def cond_kernel(got, table_hbm, xs, cond, halo, top, bottom, acc, grp, ints, lists, table, sem, sems):
    loads = []
    for r in range(R // SUBS):
        loads.append(load(table_hbm.at[:, pl.ds(r * W, W)], table.at[r], sems.at[r]))
    me = lax.axis_index("lon")
    left = lax.rem(me + PEERS - 1, PEERS)
    right = lax.rem(me + 1, PEERS)
    for d, p in enumerate((me, left, right)):
        ints[d] = got[p, CP - 16 : CP, :].astype(F32).astype(jnp.int32)
    copy = load(ints, lists, sem)
    acc[...] = jnp.zeros_like(acc)

    rows = []
    for g in range(C // EDGE):
        cols = slice(g * 32, g * 32 + 32)
        side = [got[p, HELD * CP :, cols].astype(F32) for p in (right, left)]
        rows.append(jnp.concatenate(side + [jnp.zeros((EDGE, 64), F32)], axis=1))
    both = jnp.concatenate(rows, axis=0).astype(BF)
    src = iota((LT, R * LT), 0)
    dst = iota((LT, R * LT), 1)
    at = dst % LT
    kind = jnp.where(at < 64, at, at - 124)
    wanted = ((at < 2) | (at >= 126)) & (src == kind * R + dst // LT)
    place = jnp.where(wanted, 1.0, 0.0).astype(BF)
    tiles = jnp.dot(both, place, preferred_element_type=F32).astype(BF)
    for r in range(R):
        halo[pl.ds(r * C, C), :] = tiles[:, r * LT : (r + 1) * LT]

    copy.wait()
    for d in range(3):
        for s in range(SUBS):
            for k in range(SLOTS):
                n = s * SLOTS + k
                block = lists[d, 14, n]
                part = got[block // HELD, pl.ds(pl.multiple_of(lax.rem(block, HELD) * CP, CP), CP), :]
                at = (d * SUBS + s) * (KINDS + 1) + lists[d, 14, 16 + n]
                acc[at] = acc[at] + part.astype(F32)
    for d in range(3):
        for s in range(SUBS):
            for w in range(KINDS):
                grp[d, pl.ds(s * CP, CP), w * LT : (w + 1) * LT] = acc[(d * SUBS + s) * (KINDS + 1) + w].astype(BF)

    lane = iota((SUBS * CP, LT), 1)
    for r in range(R // SUBS):
        loads[r].wait()
        own = jnp.dot(grp[0], table[r], preferred_element_type=F32).astype(BF)
        lhs = jnp.dot(grp[1], table[r, :, W - LT : W], preferred_element_type=F32)
        rhs = jnp.dot(grp[2], table[r, :, 0:LT], preferred_element_type=F32)
        side = jnp.where(lane < 2, rhs, jnp.where(lane >= 126, lhs, 0.0)).astype(BF)
        for s in range(SUBS):
            at = pl.ds((s * SUBS + r) * CP, CP)
            cond[at, 0:W] = own[s * CP : (s + 1) * CP]
            cond[at, W:WX] = side[s * CP : (s + 1) * CP]
    for out, r0 in ((top, 0), (bottom, R - 2)):
        out[0 : 2 * C, 0:W] = xs[pl.ds(r0 * C, 2 * C), :]
        out[0 : 2 * C, W:WX] = halo[pl.ds(r0 * C, 2 * C), :]
        out[2 * C : 2 * C + 2 * CP, :] = cond[pl.ds(r0 * CP, 2 * CP), :]


def cond_tile(got, table, xs):
    edge = struct((2 * (C + CP), WX))
    return pl.pallas_call(
        cond_kernel,
        out_shape=(kept((R * CP, WX)), kept((R * C, LT)), edge, edge),
        in_specs=vmem(1) + hbm(1) + vmem(1),
        out_specs=tuple(vmem(4)),
        scratch_shapes=[
            pltpu.VMEM((3 * SUBS * (KINDS + 1), CP, LT), F32),
            pltpu.VMEM((3, SUBS * CP, KINDS * LT), BF),
            pltpu.VMEM((3, 16, LT), jnp.int32),
            pltpu.SMEM((3, 16, LT), jnp.int32),
            pltpu.VMEM((R // SUBS, KINDS * LT, W), BF),
            pltpu.SemaphoreType.DMA,
            pltpu.SemaphoreType.DMA((R // SUBS,)),
        ],
        compiler_params=params(14),
    )(*in_vmem(got), *in_hbm(table), *in_vmem(xs))


def silu(v):
    return v / (1.0 + jnp.exp(-v))


def inner_kernel(hid, cond, halo, xs, wts, bias, zi, edge, c3, h3, a3):
    for r in range(R):
        for d, y in enumerate(shifted(cond[pl.ds(r * CP, CP), :], WX)):
            c3[pl.ds((r * 3 + d) * CP, CP), :] = y
        blank = jnp.zeros((C, LT), BF)
        h = jnp.concatenate([blank, halo[pl.ds(r * C, C), :], blank], axis=1)
        for d, y in enumerate(shifted(h, 3 * LT)):
            h3[pl.ds((r * 3 + d) * C, C), :] = y
    for i in range(PAIRS):
        v = jnp.dot(wts[:, 2 * TAPS :], c3[pl.ds(i * 6 * CP, 12 * CP), :], preferred_element_type=F32)
        e = jnp.dot(wts[:, 0:TAPS], h3[pl.ds(i * 6 * C, 12 * C), :], preferred_element_type=F32)
        v = v + hid[i].astype(F32)
        v = jnp.concatenate(
            [v[:, 0:LT] + e[:, 2 * LT :], v[:, LT : W - LT], v[:, W - LT :] + e[:, 0 : 2 * LT]], axis=1
        )
        a = silu(v).astype(BF)
        for j in range(2):
            r = i * 2 + j
            x = a[j * C : (j + 1) * C]
            if r < 2 or r >= R - 4:
                edge[pl.ds((r if r < 2 else r - R + 6) * C, C), :] = x
            for d, y in enumerate(shifted(x, WX)):
                a3[pl.ds((r * 3 + d) * C, C), :] = y[:, 0:W]
    for i in range(PAIRS - 1):
        y = jnp.dot(wts[:, TAPS : 2 * TAPS], a3[pl.ds(i * 6 * C, 12 * C), :], preferred_element_type=F32)
        y = y + xs[pl.ds((i + 1) * 2 * C, 2 * C), :].astype(F32) + bias[:, LT : LT + 1]
        zi[pl.ds(i * 2 * C, 2 * C), :] = y.astype(BF)


def inner_rows(hid, cond, halo, xs, wts, bias):
    return pl.pallas_call(
        inner_kernel,
        out_shape=(kept(((R - 4) * C, W)), kept((4 * C, WX))),
        in_specs=vmem(6),
        out_specs=tuple(vmem(2)),
        scratch_shapes=[
            pltpu.VMEM((R * 3 * CP, WX), BF),
            pltpu.VMEM((R * 3 * C, 3 * LT), BF),
            pltpu.VMEM(((R - 2) * 3 * C, W), BF),
        ],
        compiler_params=params(20),
        cost_estimate=pl.CostEstimate(flops=4 * 10**9, bytes_accessed=12 * 10**6, transcendentals=10**6),
    )(*in_vmem(hid, cond, halo, xs, wts, bias))


def outer_kernel(
    zi, edge, top, bottom, above, below, xs, wts, bias, out, n3, c3, a3, z, buf, sems
):
    lat = lax.axis_index("lat")
    first = jnp.where(lat == 0, 0.0, 1.0)
    last = jnp.where(lat == lax.axis_size("lat") - 1, 0.0, 1.0)

    def put(row, x):
        for d, y in enumerate(shifted(x, WX)):
            a3[pl.ds((row * 3 + d) * C, C), :] = y[:, 0:W]

    for r in range(4):
        put(2 + r, edge[pl.ds(r * C, C), :])
    for part, (lo, hi) in enumerate(((above, top), (bottom, below))):
        for r, ref in enumerate((lo, lo, hi, hi)):
            n = part * 4 + r
            for d, y in enumerate(shifted(ref[pl.ds(r % 2 * C, C), :], WX)):
                n3[pl.ds((n * 3 + d) * C, C), :] = y
            for d, y in enumerate(shifted(ref[pl.ds(2 * C + r % 2 * CP, CP), :], WX)):
                c3[pl.ds((n * 3 + d) * CP, CP), :] = y
    for part in range(2):
        v = jnp.dot(wts[:, 0:TAPS], n3[pl.ds(part * 12 * C, 12 * C), :], preferred_element_type=F32)
        v = v + jnp.dot(wts[:, 2 * TAPS :], c3[pl.ds(part * 12 * CP, 12 * CP), :], preferred_element_type=F32)
        v = silu(v + bias[:, 0:1])
        if part == 0:
            put(0, (v[0:C] * first).astype(BF))
            put(1, v[C:].astype(BF))
        else:
            put(6, v[0:C].astype(BF))
            put(7, (v[C:] * last).astype(BF))
    for part, r0 in ((0, 0), (1, R - 2)):
        at = pl.ds(r0 * C, 2 * C)
        y = jnp.dot(
            wts[:, TAPS : 2 * TAPS], a3[pl.ds(part * 12 * C, 12 * C), :], preferred_element_type=F32
        )
        z[pl.ds(part * 2 * C, 2 * C), :] = (y + xs[at, :].astype(F32) + bias[:, LT : LT + 1]).astype(BF)
    copies = []
    each = C // PARTS
    for g in range(PARTS):
        rows = [z[pl.ds(r * C + g * each, each), :] for r in range(2)]
        rows += [zi[pl.ds(r * C + g * each, each), :] for r in range(R - 4)]
        rows += [z[pl.ds(r * C + g * each, each), :] for r in range(2, 4)]
        part = pl.ds(g * each, each)
        buf[part] = jnp.swapaxes(jnp.stack(rows, axis=0), 0, 1)
        copies.append(load(buf.at[part], out.at[part], sems.at[g]))
    for copy in copies:
        copy.wait()


def outer_rows(zi, edge, top, bottom, above, below, xs, wts, bias):
    return pl.pallas_call(
        outer_kernel,
        out_shape=pltpu.HBM((C, R, W), BF),
        in_specs=vmem(9),
        out_specs=hbm(1)[0],
        scratch_shapes=[
            pltpu.VMEM((24 * C, WX), BF),
            pltpu.VMEM((24 * CP, WX), BF),
            pltpu.VMEM((24 * C, W), BF),
            pltpu.VMEM((4 * C, W), BF),
            pltpu.VMEM((C, R, W), BF),
            pltpu.SemaphoreType.DMA((PARTS,)),
        ],
        compiler_params=params(22),
    )(*in_vmem(zi, edge), top, bottom, above, below, *in_vmem(xs, wts, bias))


def local(noisy, coarse, owner, slot, weight, counts, table, conv_in, conv_cond, bias_in, conv_out, bias_out):
    coarse = jnp.transpose(coarse, (0, 2, 1, 3))
    conv_cond = jnp.transpose(conv_cond, (0, 1, 3, 2))
    table = table.reshape(KINDS * LT, table.shape[2])
    msg = message(noisy, coarse, owner, slot, weight, counts)
    got = lax.all_to_all(msg, "lon", split_axis=0, concat_axis=0, tiled=True)
    xs, hid, wts, bias = own_tile(noisy, conv_in, conv_cond, conv_out, bias_in[None], bias_out[None])
    cond, halo, top, bottom = cond_tile(got, table, xs)
    count = lax.axis_size("lat")
    above = lax.ppermute(bottom, "lat", [(i, i + 1) for i in range(count - 1)])
    below = lax.ppermute(top, "lat", [(i + 1, i) for i in range(count - 1)])
    zi, edge = inner_rows(hid, cond, halo, xs, wts, bias)
    return outer_rows(zi, edge, top, bottom, above, below, xs, wts, bias)


def solution(mesh):
    grid = P("lat", "lon")
    in_specs = (P(None, "lat", "lon"),) + (grid,) * 5 + (P(),) * 6
    return jax.shard_map(local, mesh=mesh, in_specs=in_specs, out_specs=P(None, "lat", "lon"), check_vma=False)
```

```python
import jax
import jax.numpy as jnp
from jax import lax
from jax.experimental import pallas as pl
from jax.experimental.pallas import tpu as pltpu
from jax.sharding import PartitionSpec as P

BF = jnp.bfloat16
F32 = jnp.float32
MIB = 1024 * 1024

C = 64
CP = 32
R = 16
W = 1280
LT = 128
WX = W + LT
PEERS = 16
HELD = 4
SUBS = 4
SLOTS = 4
KINDS = 4
EDGE = 16
MSG = HELD * CP + EDGE
PAIRS = R // 2 - 1
TAP = 3 * (C + CP)
TAPS = 4 * TAP
TAPS_OUT = 12 * C
PARTS = 4


def vmem(n=1):
    return [pl.BlockSpec(memory_space=pltpu.VMEM)] * n


def smem(n=1):
    return [pl.BlockSpec(memory_space=pltpu.SMEM)] * n


def params(mib):
    return pltpu.CompilerParams(vmem_limit_bytes=mib * MIB)


def struct(shape, dtype=BF):
    return jax.ShapeDtypeStruct(shape, dtype)


def kept(shape, dtype=BF):
    return pltpu.VMEM(shape, dtype)


def hbm(n=1):
    return [pl.BlockSpec(memory_space=pltpu.HBM)] * n


def in_hbm(*arrays):
    return [pltpu.with_memory_space_constraint(a, pltpu.HBM) for a in arrays]


def in_vmem(*arrays):
    return [pltpu.with_memory_space_constraint(a, pltpu.VMEM) for a in arrays]


def iota(shape, dim):
    return lax.broadcasted_iota(jnp.int32, shape, dim)


def message_kernel(noisy, coarse_hbm, ids, out, tiles, coarse, owner, slot, weight, counts, sems):
    me = lax.axis_index("lon")
    loads = [
        load(noisy.at[:, :, 0:LT], tiles.at[0], sems.at[0]),
        load(noisy.at[:, :, W - LT : W], tiles.at[1], sems.at[1]),
        load(coarse_hbm, coarse, sems.at[2]),
    ]
    loads += [load(a, b, sems.at[3 + i]) for i, (a, b) in enumerate(zip(ids, (owner, slot, weight, counts)))]
    for copy in loads:
        copy.wait()
    lane = iota((C, R, LT), 2)
    edge = jnp.where(lane < 64, tiles[0].astype(F32), tiles[1].astype(F32))
    edge = jnp.swapaxes(edge.astype(BF), 0, 1)
    edge = jnp.concatenate([edge[r] for r in range(R)], axis=1)
    row = iota((R * LT, LT), 0)
    col = iota((R * LT, LT), 1)
    at = row % LT
    kind = jnp.where(at < 64, at, at - 124)
    wanted = ((at < 2) | (at >= 126)) & (col == kind * R + row // LT)
    pick = jnp.where(wanted, 1.0, 0.0).astype(BF)
    packed = jnp.dot(edge, pick, preferred_element_type=F32)
    sides = []
    for side in range(2):
        parts = [packed[g * EDGE : (g + 1) * EDGE, side * 32 : side * 32 + 32] for g in range(C // EDGE)]
        sides.append(jnp.concatenate(parts, axis=1))
    lanes = iota((2, HELD, LT), 2)
    lists = jnp.zeros((2, HELD, LT), F32)
    for s in range(SUBS):
        live = counts[0, 0, s]
        for k in range(SLOTS):
            n = s * SLOTS + k
            block = owner[0, 0, s, k] * HELD + slot[0, 0, s, k]
            kind_id = jnp.where(k < live, weight[0, 0, s, k], KINDS)
            lists = jnp.where(lanes == n, block.astype(F32), lists)
            lists = jnp.where(lanes == 16 + n, kind_id.astype(F32), lists)
    chans = coarse[0].astype(F32)
    blocks = jnp.swapaxes(jnp.concatenate([chans, lists], axis=0), 0, 1)
    blocks = blocks.reshape(HELD * CP, LT).astype(BF)
    right = lax.rem(me + 1, PEERS)
    for p in range(PEERS):
        out[p, 0 : HELD * CP] = blocks
        out[p, HELD * CP :] = jnp.where(right == p, sides[1], sides[0]).astype(BF)


def message(noisy, coarse, *ids):
    def kernel(noisy_ref, coarse_ref, owner, slot, weight, counts, *rest):
        message_kernel(noisy_ref, coarse_ref, (owner, slot, weight, counts), *rest)

    return pl.pallas_call(
        kernel,
        out_shape=kept((PEERS, MSG, LT)),
        in_specs=hbm(6),
        out_specs=vmem()[0],
        scratch_shapes=[pltpu.VMEM((2, C, R, LT), BF), pltpu.VMEM(coarse.shape, BF)]
        + [pltpu.SMEM(a.shape, jnp.int32) for a in ids]
        + [pltpu.SemaphoreType.DMA((7,))],
        compiler_params=params(12),
    )(*in_hbm(noisy, coarse, *ids))


def load(src, dst, sem):
    copy = pltpu.make_async_copy(src, dst, sem)
    copy.start()
    return copy


def shifted(x, width):
    return [pltpu.roll(x, 1, 1), x, pltpu.roll(x, width - 1, 1)]


def pair_weights(taps):
    rows = jnp.concatenate(taps, axis=1)
    blank = jnp.zeros((rows.shape[0], rows.shape[1] // 3), BF)
    return jnp.concatenate(
        [jnp.concatenate([rows, blank], axis=1), jnp.concatenate([blank, rows], axis=1)], axis=0
    )


def cond_tap(tap):
    tap = jnp.concatenate([tap.astype(F32), jnp.zeros((CP - tap.shape[0], tap.shape[1]), F32)], axis=0)
    return tap.T.astype(BF)


def bias_column(row):
    same = iota((C, C), 0) == iota((C, C), 1)
    column = jnp.sum(jnp.where(same, row, 0.0), axis=1, keepdims=True)
    return jnp.concatenate([column, column], axis=0)


def near_rows():
    odd = lax.rem(lax.axis_index("lat"), 2)
    return (1 - odd) * (R - 2), odd * (R - 2)


def turn_kernel(
    noisy, conv_in, conv_cond, conv_out, bias_in, bias_out, xs, first, second, wts_hbm, bias_hbm, buf, wts, bias, sems
):
    loads = []
    for g in range(PARTS):
        part = pl.ds(g * (C // PARTS), C // PARTS)
        loads.append(load(noisy.at[part], buf.at[part], sems.at[g]))
    taps = []
    for i in range(3):
        taps += [conv_in[i, j] for j in range(3)] + [cond_tap(conv_cond[i, j]) for j in range(3)]
    wts[:, 0:TAPS] = pair_weights(taps)
    wts[:, TAPS:] = pair_weights([conv_out[i, j] for i in range(3) for j in range(3)])
    bias[:, 0:LT] = jnp.broadcast_to(bias_column(bias_in[...]), (2 * C, LT))
    bias[:, LT:] = jnp.broadcast_to(bias_column(bias_out[...]), (2 * C, LT))
    stores = [load(wts, wts_hbm, sems.at[PARTS]), load(bias, bias_hbm, sems.at[PARTS + 1])]
    for copy in loads:
        copy.wait()
    xs[...] = jnp.swapaxes(buf[...], 0, 1).reshape(R * C, W)
    for i, (out, r0) in enumerate(zip((first, second), near_rows())):
        rows = pl.ds(pl.multiple_of(r0 * C, C), 2 * C)
        stores.append(load(xs.at[rows], out, sems.at[PARTS + 2 + i]))
    for copy in stores:
        copy.wait()


def turned(noisy, conv_in, conv_cond, conv_out, bias_in, bias_out):
    return pl.pallas_call(
        turn_kernel,
        out_shape=(
            kept((R * C, W)),
            pltpu.HBM((2 * C, W), BF),
            pltpu.HBM((2 * C, W), BF),
            pltpu.HBM((2 * C, TAPS + TAPS_OUT), BF),
            pltpu.HBM((2 * C, 2 * LT), F32),
        ),
        in_specs=hbm(1) + vmem(5),
        out_specs=tuple(vmem(1) + hbm(4)),
        scratch_shapes=[
            pltpu.VMEM((C, R, W), BF),
            pltpu.VMEM((2 * C, TAPS + TAPS_OUT), BF),
            pltpu.VMEM((2 * C, 2 * LT), F32),
            pltpu.SemaphoreType.DMA((PARTS + 4,)),
        ],
        compiler_params=params(10),
        cost_estimate=pl.CostEstimate(flops=3 * 10**9, bytes_accessed=12 * 10**6, transcendentals=0),
    )(*in_hbm(noisy, conv_in, conv_cond, conv_out, bias_in, bias_out))


def cond_kernel(got, table_hbm, wts_hbm, bias_hbm, cond, halo, first, second, wts, bias, acc, grp, ints, lists, table, sem, sems):
    loads = []
    for r in range(R // SUBS):
        loads.append(load(table_hbm.at[:, pl.ds(r * W, W)], table.at[r], sems.at[r]))
    others = [load(wts_hbm, wts, sems.at[R // SUBS]), load(bias_hbm, bias, sems.at[R // SUBS + 1])]
    me = lax.axis_index("lon")
    left = lax.rem(me + PEERS - 1, PEERS)
    right = lax.rem(me + 1, PEERS)
    for d, p in enumerate((me, left, right)):
        ints[d] = got[p, CP - 16 : CP, :].astype(F32).astype(jnp.int32)
    copy = load(ints, lists, sem)
    acc[...] = jnp.zeros_like(acc)

    rows = []
    for g in range(C // EDGE):
        cols = slice(g * 32, g * 32 + 32)
        side = [got[p, HELD * CP :, cols].astype(F32) for p in (right, left)]
        rows.append(jnp.concatenate(side + [jnp.zeros((EDGE, 64), F32)], axis=1))
    both = jnp.concatenate(rows, axis=0).astype(BF)
    src = iota((LT, R * LT), 0)
    dst = iota((LT, R * LT), 1)
    at = dst % LT
    kind = jnp.where(at < 64, at, at - 124)
    wanted = ((at < 2) | (at >= 126)) & (src == kind * R + dst // LT)
    place = jnp.where(wanted, 1.0, 0.0).astype(BF)
    tiles = jnp.dot(both, place, preferred_element_type=F32).astype(BF)
    for r in range(R):
        halo[pl.ds(r * C, C), :] = tiles[:, r * LT : (r + 1) * LT]

    copy.wait()
    for d in range(3):
        for s in range(SUBS):
            for k in range(SLOTS):
                n = s * SLOTS + k
                block = lists[d, 14, n]
                part = got[block // HELD, pl.ds(pl.multiple_of(lax.rem(block, HELD) * CP, CP), CP), :]
                at = (d * SUBS + s) * (KINDS + 1) + lists[d, 14, 16 + n]
                acc[at] = acc[at] + part.astype(F32)
    for d in range(3):
        for s in range(SUBS):
            for w in range(KINDS):
                grp[d, pl.ds(s * CP, CP), w * LT : (w + 1) * LT] = acc[(d * SUBS + s) * (KINDS + 1) + w].astype(BF)

    lane = iota((SUBS * CP, LT), 1)
    for r in range(R // SUBS):
        loads[r].wait()
        part = table.at[r]
        own = jnp.dot(grp[0], part[...], preferred_element_type=F32).astype(BF)
        lhs = jnp.dot(grp[1], part[:, W - LT : W], preferred_element_type=F32)
        rhs = jnp.dot(grp[2], part[:, 0:LT], preferred_element_type=F32)
        side = jnp.where(lane < 2, rhs, jnp.where(lane >= 126, lhs, 0.0)).astype(BF)
        for s in range(SUBS):
            at = pl.ds((s * SUBS + r) * CP, CP)
            cond[at, 0:W] = own[s * CP : (s + 1) * CP]
            cond[at, W:WX] = side[s * CP : (s + 1) * CP]
    for out, r0 in zip((first, second), near_rows()):
        out[:, 0:WX] = cond[pl.ds(pl.multiple_of(r0 * CP, CP), 2 * CP), :]
        for j in range(2):
            out[:, WX + j * LT : WX + (j + 1) * LT] = halo[pl.ds(pl.multiple_of((r0 + j) * C, C), C), :]
    for copy in others:
        copy.wait()


def cond_tile(got, table, wts, bias):
    edge = struct((2 * CP, WX + 2 * LT))
    return pl.pallas_call(
        cond_kernel,
        out_shape=(
            kept((R * CP, WX)),
            kept((R * C, LT)),
            edge,
            edge,
            kept(wts.shape),
            kept(bias.shape, F32),
        ),
        in_specs=vmem(1) + hbm(3),
        out_specs=tuple(vmem(6)),
        scratch_shapes=[
            pltpu.VMEM((3 * SUBS * (KINDS + 1), CP, LT), F32),
            pltpu.VMEM((3, SUBS * CP, KINDS * LT), BF),
            pltpu.VMEM((3, 16, LT), jnp.int32),
            pltpu.SMEM((3, 16, LT), jnp.int32),
            pltpu.VMEM((R // SUBS, KINDS * LT, W), BF),
            pltpu.SemaphoreType.DMA,
            pltpu.SemaphoreType.DMA((R // SUBS + 2,)),
        ],
        compiler_params=params(14),
    )(*in_vmem(got), *in_hbm(table, wts, bias))


def silu(v):
    return v / (1.0 + jnp.exp(-v))


def put_taps(dst, row, noisy, cond):
    at = row * TAP
    for d, y in enumerate(shifted(noisy, WX)):
        dst[pl.ds(at + d * C, C), :] = y
    for d, y in enumerate(shifted(cond, WX)):
        dst[pl.ds(at + 3 * C + d * CP, CP), :] = y


def put_act(dst, row, x):
    for d, y in enumerate(shifted(x, WX)):
        dst[pl.ds((row * 3 + d) * C, C), :] = y[:, 0:W]


def own_row(xs, halo, r):
    return jnp.concatenate([xs[pl.ds(r * C, C), :], halo[pl.ds(r * C, C), :]], axis=1)


def first_conv(wts, bias, rows):
    return silu(jnp.dot(wts[:, 0:TAPS], rows, preferred_element_type=F32) + bias[:, 0:1])


def second_conv(wts, bias, rows, x):
    y = jnp.dot(wts[:, TAPS:], rows, preferred_element_type=F32)
    return (y + x.astype(F32) + bias[:, LT : LT + 1]).astype(BF)


def inner_kernel(cond, halo, xs, wts, bias, zi, edge, x3, a3):
    for r in range(R):
        put_taps(x3, r, own_row(xs, halo, r), cond[pl.ds(r * CP, CP), :])
    for i in range(PAIRS):
        a = first_conv(wts, bias, x3[pl.ds(2 * i * TAP, TAPS), :]).astype(BF)
        for j in range(2):
            r = i * 2 + j
            x = a[j * C : (j + 1) * C]
            if r < 2 or r >= R - 4:
                edge[pl.ds((r if r < 2 else r - R + 6) * C, C), :] = x
            put_act(a3, r, x)
    for i in range(PAIRS - 1):
        x = xs[pl.ds((i + 1) * 2 * C, 2 * C), :]
        zi[pl.ds(i * 2 * C, 2 * C), :] = second_conv(wts, bias, a3[pl.ds(i * 6 * C, TAPS_OUT), :], x)


def inner_rows(cond, halo, xs, wts, bias):
    return pl.pallas_call(
        inner_kernel,
        out_shape=(kept(((R - 4) * C, W)), kept((4 * C, WX))),
        in_specs=vmem(5),
        out_specs=tuple(vmem(2)),
        scratch_shapes=[
            pltpu.VMEM((R * TAP, WX), BF),
            pltpu.VMEM(((R - 2) * 3 * C, W), BF),
        ],
        compiler_params=params(26),
        cost_estimate=pl.CostEstimate(flops=6 * 10**9, bytes_accessed=12 * 10**6, transcendentals=10**6),
    )(*in_vmem(cond, halo, xs, wts, bias))


def outer_kernel(
    zi, edge, cond, halo, noisy_1, noisy_hbm, got_1, got_2, xs, wts, bias, out, x3, a3, buf, noisy_2, sems
):
    near = load(noisy_hbm, noisy_2, sems.at[2 * PARTS])
    lat = lax.axis_index("lat")
    first = jnp.where(lat == 0, 0.0, 1.0)
    last = jnp.where(lat == lax.axis_size("lat") - 1, 0.0, 1.0)
    half = R // 2
    each = C // PARTS
    copies = []
    odd = lax.rem(lat, 2) == 1
    for part in range(2):
        put_act(a3, part * 4 + 2 - part * 2, edge[pl.ds(part * 2 * C, C), :])
        put_act(a3, part * 4 + 3 - part * 2, edge[pl.ds((part * 2 + 1) * C, C), :])
        for j in range(2):
            r = part * (R - 2) + j
            put_taps(x3, part * 4 + 2 - part * 2 + j, own_row(xs, halo, r), cond[pl.ds(r * CP, CP), :])
    near.wait()
    for part in range(2):
        for j in range(2):
            mine = odd if part == 0 else ~odd
            n = jnp.where(mine, noisy_1[pl.ds(j * C, C), :], noisy_2[pl.ds(j * C, C), :])
            far = jnp.where(mine, got_1[...], got_2[...])
            n = jnp.concatenate([n, far[:, WX + j * LT : WX + (j + 1) * LT]], axis=1)
            put_taps(x3, part * 6 + j, n, far[j * CP : (j + 1) * CP, 0:WX])
        v = first_conv(wts, bias, x3[pl.ds(part * TAPS, TAPS), :])
        if part == 0:
            put_act(a3, 0, (v[0:C] * first).astype(BF))
            put_act(a3, 1, v[C:].astype(BF))
        else:
            put_act(a3, 6, v[0:C].astype(BF))
            put_act(a3, 7, (v[C:] * last).astype(BF))
        z = second_conv(wts, bias, a3[pl.ds(part * TAPS_OUT, TAPS_OUT), :], xs[pl.ds(part * (R - 2) * C, 2 * C), :])
        rows = [z[0:C], z[C:]]
        inner = [zi[pl.ds((part * (half - 2) + r) * C, C), :] for r in range(half - 2)]
        rows = inner + rows if part else rows + inner
        here = pl.ds(part * half, half)
        for g in range(PARTS):
            chans = pl.ds(g * each, each)
            group = jnp.stack([row[g * each : (g + 1) * each] for row in rows], axis=0)
            buf[chans, here, :] = jnp.swapaxes(group, 0, 1)
            sem = sems.at[part * PARTS + g]
            copies.append(load(buf.at[chans, here, :], out.at[chans, here, :], sem))
    for copy in copies:
        copy.wait()


def outer_rows(zi, edge, cond, halo, noisy_1, noisy_2, got_1, got_2, xs, wts, bias):
    return pl.pallas_call(
        outer_kernel,
        out_shape=pltpu.HBM((C, R, W), BF),
        in_specs=vmem(5) + hbm(1) + vmem(5),
        out_specs=hbm(1)[0],
        scratch_shapes=[
            pltpu.VMEM((2 * TAPS, WX), BF),
            pltpu.VMEM((2 * TAPS_OUT, W), BF),
            pltpu.VMEM((C, R, W), BF),
            pltpu.VMEM((2 * C, W), BF),
            pltpu.SemaphoreType.DMA((2 * PARTS + 1,)),
        ],
        compiler_params=params(24),
    )(*in_vmem(zi, edge, cond, halo), noisy_1, *in_hbm(noisy_2), got_1, got_2, *in_vmem(xs, wts, bias))


def exchanged(first, second):
    count = lax.axis_size("lat")
    got_1 = lax.ppermute(first, "lat", [(i, i ^ 1) for i in range(count)])
    got_2 = lax.ppermute(second, "lat", [(i, ((i + 1) ^ 1) - 1) for i in range(1, count - 1)])
    return got_1, got_2


def local(noisy, coarse, owner, slot, weight, counts, table, conv_in, conv_cond, bias_in, conv_out, bias_out):
    coarse = jnp.transpose(coarse, (0, 2, 1, 3))
    conv_cond = jnp.transpose(conv_cond, (0, 1, 3, 2))
    table = table.reshape(KINDS * LT, table.shape[2])
    msg = message(noisy, coarse, owner, slot, weight, counts)
    got = lax.all_to_all(msg, "lon", split_axis=0, concat_axis=0, tiled=True)
    xs, first, second, wts, bias = turned(noisy, conv_in, conv_cond, conv_out, bias_in[None], bias_out[None])
    noisy_1, noisy_2 = exchanged(first, second)
    cond, halo, first, second, wts, bias = cond_tile(got, table, wts, bias)
    got_1, got_2 = exchanged(first, second)
    zi, edge = inner_rows(cond, halo, xs, wts, bias)
    return outer_rows(zi, edge, cond, halo, noisy_1, noisy_2, got_1, got_2, xs, wts, bias)


def solution(mesh):
    grid = P("lat", "lon")
    in_specs = (P(None, "lat", "lon"),) + (grid,) * 5 + (P(),) * 6
    return jax.shard_map(local, mesh=mesh, in_specs=in_specs, out_specs=P(None, "lat", "lon"), check_vma=False)
```

```python
import jax
import jax.numpy as jnp
from jax import lax
from jax.experimental import pallas as pl
from jax.experimental.pallas import tpu as pltpu
from jax.sharding import PartitionSpec as P

BF = jnp.bfloat16
F32 = jnp.float32
MIB = 1024 * 1024

C = 64
CP = 32
R = 16
W = 1280
LT = 128
WX = W + LT
PEERS = 16
HELD = 4
SUBS = 4
SLOTS = 4
KINDS = 4
EDGE = 16
MSG = HELD * CP + EDGE
PAIRS = R // 2 - 1
TAP = 3 * (C + CP)
TAPS = 4 * TAP
TAPS_OUT = 12 * C
PARTS = 4


def vmem(n=1):
    return [pl.BlockSpec(memory_space=pltpu.VMEM)] * n


def smem(n=1):
    return [pl.BlockSpec(memory_space=pltpu.SMEM)] * n


def params(mib):
    return pltpu.CompilerParams(vmem_limit_bytes=mib * MIB)


def struct(shape, dtype=BF):
    return jax.ShapeDtypeStruct(shape, dtype)


def kept(shape, dtype=BF):
    return pltpu.VMEM(shape, dtype)


def hbm(n=1):
    return [pl.BlockSpec(memory_space=pltpu.HBM)] * n


def in_hbm(*arrays):
    return [pltpu.with_memory_space_constraint(a, pltpu.HBM) for a in arrays]


def in_vmem(*arrays):
    return [pltpu.with_memory_space_constraint(a, pltpu.VMEM) for a in arrays]


def iota(shape, dim):
    return lax.broadcasted_iota(jnp.int32, shape, dim)


def message_kernel(noisy, coarse_hbm, ids, out, tiles, coarse, owner, slot, weight, counts, sems):
    me = lax.axis_index("lon")
    loads = [
        load(noisy.at[:, :, 0:LT], tiles.at[0], sems.at[0]),
        load(noisy.at[:, :, W - LT : W], tiles.at[1], sems.at[1]),
        load(coarse_hbm, coarse, sems.at[2]),
    ]
    loads += [load(a, b, sems.at[3 + i]) for i, (a, b) in enumerate(zip(ids, (owner, slot, weight, counts)))]
    for copy in loads:
        copy.wait()
    lane = iota((C, R, LT), 2)
    edge = jnp.where(lane < 64, tiles[0].astype(F32), tiles[1].astype(F32))
    edge = jnp.swapaxes(edge.astype(BF), 0, 1)
    edge = jnp.concatenate([edge[r] for r in range(R)], axis=1)
    row = iota((R * LT, LT), 0)
    col = iota((R * LT, LT), 1)
    at = row % LT
    kind = jnp.where(at < 64, at, at - 124)
    wanted = ((at < 2) | (at >= 126)) & (col == kind * R + row // LT)
    pick = jnp.where(wanted, 1.0, 0.0).astype(BF)
    packed = jnp.dot(edge, pick, preferred_element_type=F32)
    sides = []
    for side in range(2):
        parts = [packed[g * EDGE : (g + 1) * EDGE, side * 32 : side * 32 + 32] for g in range(C // EDGE)]
        sides.append(jnp.concatenate(parts, axis=1))
    lanes = iota((2, HELD, LT), 2)
    lists = jnp.zeros((2, HELD, LT), F32)
    for s in range(SUBS):
        live = counts[0, 0, s]
        for k in range(SLOTS):
            n = s * SLOTS + k
            block = owner[0, 0, s, k] * HELD + slot[0, 0, s, k]
            kind_id = jnp.where(k < live, weight[0, 0, s, k], KINDS)
            lists = jnp.where(lanes == n, block.astype(F32), lists)
            lists = jnp.where(lanes == 16 + n, kind_id.astype(F32), lists)
    chans = coarse[0].astype(F32)
    blocks = jnp.swapaxes(jnp.concatenate([chans, lists], axis=0), 0, 1)
    blocks = blocks.reshape(HELD * CP, LT).astype(BF)
    right = lax.rem(me + 1, PEERS)
    for p in range(PEERS):
        out[p, 0 : HELD * CP] = blocks
        out[p, HELD * CP :] = jnp.where(right == p, sides[1], sides[0]).astype(BF)


def message(noisy, coarse, *ids):
    def kernel(noisy_ref, coarse_ref, owner, slot, weight, counts, *rest):
        message_kernel(noisy_ref, coarse_ref, (owner, slot, weight, counts), *rest)

    return pl.pallas_call(
        kernel,
        out_shape=kept((PEERS, MSG, LT)),
        in_specs=hbm(6),
        out_specs=vmem()[0],
        scratch_shapes=[pltpu.VMEM((2, C, R, LT), BF), pltpu.VMEM(coarse.shape, BF)]
        + [pltpu.SMEM(a.shape, jnp.int32) for a in ids]
        + [pltpu.SemaphoreType.DMA((7,))],
        compiler_params=params(12),
    )(*in_hbm(noisy, coarse, *ids))


def load(src, dst, sem):
    copy = pltpu.make_async_copy(src, dst, sem)
    copy.start()
    return copy


def shifted(x, width):
    return [pltpu.roll(x, 1, 1), x, pltpu.roll(x, width - 1, 1)]


def pair_weights(taps):
    rows = jnp.concatenate(taps, axis=1)
    blank = jnp.zeros((rows.shape[0], rows.shape[1] // 3), BF)
    return jnp.concatenate(
        [jnp.concatenate([rows, blank], axis=1), jnp.concatenate([blank, rows], axis=1)], axis=0
    )


def cond_tap(tap):
    tap = jnp.concatenate([tap.astype(F32), jnp.zeros((CP - tap.shape[0], tap.shape[1]), F32)], axis=0)
    return tap.T.astype(BF)


def bias_column(row):
    same = iota((C, C), 0) == iota((C, C), 1)
    column = jnp.sum(jnp.where(same, row, 0.0), axis=1, keepdims=True)
    return jnp.concatenate([column, column], axis=0)


def near_rows():
    odd = lax.rem(lax.axis_index("lat"), 2)
    return (1 - odd) * (R - 2), odd * (R - 2)


def turn_kernel(
    noisy, params_hbm, xs, first, second, wts_hbm, bias_hbm, buf, wts, bias, small, sems, small_sems
):
    small_loads = [load(a, b, small_sems.at[i]) for i, (a, b) in enumerate(zip(params_hbm, small))]
    conv_in, conv_cond, conv_out, bias_in, bias_out = small
    loads = []
    for g in range(PARTS):
        part = pl.ds(g * (C // PARTS), C // PARTS)
        loads.append(load(noisy.at[part], buf.at[part], sems.at[g]))
    for copy in small_loads:
        copy.wait()
    taps = []
    for i in range(3):
        taps += [conv_in[i, j] for j in range(3)] + [cond_tap(conv_cond[i, j]) for j in range(3)]
    wts[:, 0:TAPS] = pair_weights(taps)
    wts[:, TAPS:] = pair_weights([conv_out[i, j] for i in range(3) for j in range(3)])
    bias[:, 0:LT] = jnp.broadcast_to(bias_column(bias_in[...]), (2 * C, LT))
    bias[:, LT:] = jnp.broadcast_to(bias_column(bias_out[...]), (2 * C, LT))
    stores = [load(wts, wts_hbm, sems.at[PARTS]), load(bias, bias_hbm, sems.at[PARTS + 1])]
    for copy in loads:
        copy.wait()
    xs[...] = jnp.swapaxes(buf[...], 0, 1).reshape(R * C, W)
    for i, (out, r0) in enumerate(zip((first, second), near_rows())):
        rows = pl.ds(pl.multiple_of(r0 * C, C), 2 * C)
        stores.append(load(xs.at[rows], out, sems.at[PARTS + 2 + i]))
    for copy in stores:
        copy.wait()


def turned(noisy, *small):
    count = len(small)

    def kernel(noisy_ref, *refs):
        scratch = refs[count + 5 :]
        turn_kernel(
            noisy_ref, refs[:count], *refs[count : count + 5], *scratch[:3], scratch[3 : 3 + count], *scratch[3 + count :]
        )

    return pl.pallas_call(
        kernel,
        out_shape=(
            kept((R * C, W)),
            pltpu.HBM((2 * C, W), BF),
            pltpu.HBM((2 * C, W), BF),
            pltpu.HBM((2 * C, TAPS + TAPS_OUT), BF),
            pltpu.HBM((2 * C, 2 * LT), F32),
        ),
        in_specs=hbm(1 + count),
        out_specs=tuple(vmem(1) + hbm(4)),
        scratch_shapes=[
            pltpu.VMEM((C, R, W), BF),
            pltpu.VMEM((2 * C, TAPS + TAPS_OUT), BF),
            pltpu.VMEM((2 * C, 2 * LT), F32),
        ]
        + [pltpu.VMEM(a.shape, a.dtype) for a in small]
        + [pltpu.SemaphoreType.DMA((PARTS + 4,)), pltpu.SemaphoreType.DMA((count,))],
        compiler_params=params(10),
        cost_estimate=pl.CostEstimate(flops=3 * 10**9, bytes_accessed=12 * 10**6, transcendentals=0),
    )(*in_hbm(noisy, *small))


def cond_kernel(got, table_hbm, wts_hbm, bias_hbm, cond, halo, first, second, wts, bias, acc, grp, ints, lists, table, sem, sems):
    loads = []
    for r in range(R // SUBS):
        loads.append(load(table_hbm.at[:, pl.ds(r * W, W)], table.at[r], sems.at[r]))
    others = [load(wts_hbm, wts, sems.at[R // SUBS]), load(bias_hbm, bias, sems.at[R // SUBS + 1])]
    me = lax.axis_index("lon")
    left = lax.rem(me + PEERS - 1, PEERS)
    right = lax.rem(me + 1, PEERS)
    for d, p in enumerate((me, left, right)):
        ints[d] = got[p, CP - 16 : CP, :].astype(F32).astype(jnp.int32)
    copy = load(ints, lists, sem)
    acc[...] = jnp.zeros_like(acc)

    rows = []
    for g in range(C // EDGE):
        cols = slice(g * 32, g * 32 + 32)
        side = [got[p, HELD * CP :, cols].astype(F32) for p in (right, left)]
        rows.append(jnp.concatenate(side + [jnp.zeros((EDGE, 64), F32)], axis=1))
    both = jnp.concatenate(rows, axis=0).astype(BF)
    src = iota((LT, R * LT), 0)
    dst = iota((LT, R * LT), 1)
    at = dst % LT
    kind = jnp.where(at < 64, at, at - 124)
    wanted = ((at < 2) | (at >= 126)) & (src == kind * R + dst // LT)
    place = jnp.where(wanted, 1.0, 0.0).astype(BF)
    tiles = jnp.dot(both, place, preferred_element_type=F32).astype(BF)
    for r in range(R):
        halo[pl.ds(r * C, C), :] = tiles[:, r * LT : (r + 1) * LT]

    copy.wait()
    for d in range(3):
        for s in range(SUBS):
            for k in range(SLOTS):
                n = s * SLOTS + k
                block = lists[d, 14, n]
                part = got[block // HELD, pl.ds(pl.multiple_of(lax.rem(block, HELD) * CP, CP), CP), :]
                at = (d * SUBS + s) * (KINDS + 1) + lists[d, 14, 16 + n]
                acc[at] = acc[at] + part.astype(F32)
    for d in range(3):
        for s in range(SUBS):
            for w in range(KINDS):
                grp[d, pl.ds(s * CP, CP), w * LT : (w + 1) * LT] = acc[(d * SUBS + s) * (KINDS + 1) + w].astype(BF)

    lane = iota((SUBS * CP, LT), 1)
    for r in range(R // SUBS):
        loads[r].wait()
        part = table.at[r]
        own = jnp.dot(grp[0], part[...], preferred_element_type=F32).astype(BF)
        lhs = jnp.dot(grp[1], part[:, W - LT : W], preferred_element_type=F32)
        rhs = jnp.dot(grp[2], part[:, 0:LT], preferred_element_type=F32)
        side = jnp.where(lane < 2, rhs, jnp.where(lane >= 126, lhs, 0.0)).astype(BF)
        for s in range(SUBS):
            at = pl.ds((s * SUBS + r) * CP, CP)
            cond[at, 0:W] = own[s * CP : (s + 1) * CP]
            cond[at, W:WX] = side[s * CP : (s + 1) * CP]
    for out, r0 in zip((first, second), near_rows()):
        out[:, 0:WX] = cond[pl.ds(pl.multiple_of(r0 * CP, CP), 2 * CP), :]
        for j in range(2):
            out[:, WX + j * LT : WX + (j + 1) * LT] = halo[pl.ds(pl.multiple_of((r0 + j) * C, C), C), :]
    for copy in others:
        copy.wait()


def cond_tile(got, table, wts, bias):
    edge = struct((2 * CP, WX + 2 * LT))
    return pl.pallas_call(
        cond_kernel,
        out_shape=(
            kept((R * CP, WX)),
            kept((R * C, LT)),
            edge,
            edge,
            kept(wts.shape),
            kept(bias.shape, F32),
        ),
        in_specs=vmem(1) + hbm(3),
        out_specs=tuple(vmem(6)),
        scratch_shapes=[
            pltpu.VMEM((3 * SUBS * (KINDS + 1), CP, LT), F32),
            pltpu.VMEM((3, SUBS * CP, KINDS * LT), BF),
            pltpu.VMEM((3, 16, LT), jnp.int32),
            pltpu.SMEM((3, 16, LT), jnp.int32),
            pltpu.VMEM((R // SUBS, KINDS * LT, W), BF),
            pltpu.SemaphoreType.DMA,
            pltpu.SemaphoreType.DMA((R // SUBS + 2,)),
        ],
        compiler_params=params(14),
    )(*in_vmem(got), *in_hbm(table, wts, bias))


def silu(v):
    return v / (1.0 + jnp.exp(-v))


def put_taps(dst, row, noisy, cond):
    at = row * TAP
    for d, y in enumerate(shifted(noisy, WX)):
        dst[pl.ds(at + d * C, C), :] = y
    for d, y in enumerate(shifted(cond, WX)):
        dst[pl.ds(at + 3 * C + d * CP, CP), :] = y


def put_act(dst, row, x):
    for d, y in enumerate(shifted(x, WX)):
        dst[pl.ds((row * 3 + d) * C, C), :] = y[:, 0:W]


def own_row(xs, halo, r):
    return jnp.concatenate([xs[pl.ds(r * C, C), :], halo[pl.ds(r * C, C), :]], axis=1)


def first_conv(wts, bias, rows):
    return silu(jnp.dot(wts[:, 0:TAPS], rows, preferred_element_type=F32) + bias[:, 0:1])


def second_conv(wts, bias, rows, x):
    y = jnp.dot(wts[:, TAPS:], rows, preferred_element_type=F32)
    return (y + x.astype(F32) + bias[:, LT : LT + 1]).astype(BF)


def inner_kernel(cond, halo, xs, wts, bias, zi, edge, x3, a3):
    for r in range(R):
        put_taps(x3, r, own_row(xs, halo, r), cond[pl.ds(r * CP, CP), :])
    for i in range(PAIRS):
        a = first_conv(wts, bias, x3[pl.ds(2 * i * TAP, TAPS), :]).astype(BF)
        for j in range(2):
            r = i * 2 + j
            x = a[j * C : (j + 1) * C]
            if r < 2 or r >= R - 4:
                edge[pl.ds((r if r < 2 else r - R + 6) * C, C), :] = x
            put_act(a3, r, x)
    for i in range(PAIRS - 1):
        x = xs[pl.ds((i + 1) * 2 * C, 2 * C), :]
        zi[pl.ds(i * 2 * C, 2 * C), :] = second_conv(wts, bias, a3[pl.ds(i * 6 * C, TAPS_OUT), :], x)


def inner_rows(cond, halo, xs, wts, bias):
    return pl.pallas_call(
        inner_kernel,
        out_shape=(kept(((R - 4) * C, W)), kept((4 * C, WX))),
        in_specs=vmem(5),
        out_specs=tuple(vmem(2)),
        scratch_shapes=[
            pltpu.VMEM((R * TAP, WX), BF),
            pltpu.VMEM(((R - 2) * 3 * C, W), BF),
        ],
        compiler_params=params(26),
        cost_estimate=pl.CostEstimate(flops=6 * 10**9, bytes_accessed=12 * 10**6, transcendentals=10**6),
    )(*in_vmem(cond, halo, xs, wts, bias))


def outer_kernel(
    zi, edge, cond, halo, noisy_1, noisy_hbm, got_1, got_2, xs, wts, bias, out, x3, a3, buf, noisy_2, sems
):
    lat = lax.axis_index("lat")
    half = R // 2
    each = C // PARTS
    upper = jnp.where(lat == 0, 0.0, 1.0)
    lower = jnp.where(lat == lax.axis_size("lat") - 1, 0.0, 1.0)

    def both_sides(odd):
        near = load(noisy_hbm, noisy_2, sems.at[2 * PARTS])
        copies = []
        sides = ((1 - odd, got_1), (odd, got_2))
        for k, (low, _) in enumerate(sides):
            for j in range(2):
                put_act(a3.at[k], (1 - low) * 2 + j, edge[pl.ds((low * 2 + j) * C, C), :])
                r = low * (R - 2) + j
                put_taps(x3.at[k], (1 - low) * 2 + j, own_row(xs, halo, r), cond[pl.ds(r * CP, CP), :])
        for k, (low, got) in enumerate(sides):
            if k == 1:
                near.wait()
            noisy = noisy_2 if k else noisy_1
            for j in range(2):
                tile = got[:, WX + j * LT : WX + (j + 1) * LT]
                x = jnp.concatenate([noisy[pl.ds(j * C, C), :], tile], axis=1)
                put_taps(x3.at[k], low * 2 + j, x, got[j * CP : (j + 1) * CP, 0:WX])
            v = first_conv(wts, bias, x3[k])
            v0, v1 = (v[0:C], v[C:] * lower) if low else (v[0:C] * upper, v[C:])
            put_act(a3.at[k], low * 2, v0.astype(BF))
            put_act(a3.at[k], low * 2 + 1, v1.astype(BF))
            z = second_conv(wts, bias, a3[k], xs[pl.ds(low * (R - 2) * C, 2 * C), :])
            rows = [z[0:C], z[C:]]
            inner = [zi[pl.ds((low * (half - 2) + r) * C, C), :] for r in range(half - 2)]
            rows = inner + rows if low else rows + inner
            here = pl.ds(low * half, half)
            for g in range(PARTS):
                chans = pl.ds(g * each, each)
                group = jnp.stack([row[g * each : (g + 1) * each] for row in rows], axis=0)
                buf[k, chans] = jnp.swapaxes(group, 0, 1)
                copies.append(load(buf.at[k, chans], out.at[chans, here, :], sems.at[k * PARTS + g]))
        for copy in copies:
            copy.wait()

    for odd in range(2):
        pl.when(lax.rem(lat, 2) == odd)(lambda odd=odd: both_sides(odd))


def outer_rows(zi, edge, cond, halo, noisy_1, noisy_2, got_1, got_2, xs, wts, bias):
    return pl.pallas_call(
        outer_kernel,
        out_shape=pltpu.HBM((C, R, W), BF),
        in_specs=vmem(5) + hbm(1) + vmem(5),
        out_specs=hbm(1)[0],
        scratch_shapes=[
            pltpu.VMEM((2, TAPS, WX), BF),
            pltpu.VMEM((2, TAPS_OUT, W), BF),
            pltpu.VMEM((2, C, R // 2, W), BF),
            pltpu.VMEM((2 * C, W), BF),
            pltpu.SemaphoreType.DMA((2 * PARTS + 1,)),
        ],
        compiler_params=params(24),
    )(*in_vmem(zi, edge, cond, halo), noisy_1, *in_hbm(noisy_2), got_1, got_2, *in_vmem(xs, wts, bias))


def exchanged(first, second):
    count = lax.axis_size("lat")
    got_1 = lax.ppermute(first, "lat", [(i, i ^ 1) for i in range(count)])
    got_2 = lax.ppermute(second, "lat", [(i, ((i + 1) ^ 1) - 1) for i in range(1, count - 1)])
    return got_1, got_2


def local(noisy, coarse, owner, slot, weight, counts, table, conv_in, conv_cond, bias_in, conv_out, bias_out):
    coarse = jnp.transpose(coarse, (0, 2, 1, 3))
    conv_cond = jnp.transpose(conv_cond, (0, 1, 3, 2))
    table = table.reshape(KINDS * LT, table.shape[2])
    msg = message(noisy, coarse, owner, slot, weight, counts)
    got = lax.all_to_all(msg, "lon", split_axis=0, concat_axis=0, tiled=True)
    xs, first, second, wts, bias = turned(noisy, conv_in, conv_cond, conv_out, bias_in[None], bias_out[None])
    noisy_1, noisy_2 = exchanged(first, second)
    cond, halo, first, second, wts, bias = cond_tile(got, table, wts, bias)
    got_1, got_2 = exchanged(first, second)
    zi, edge = inner_rows(cond, halo, xs, wts, bias)
    return outer_rows(zi, edge, cond, halo, noisy_1, noisy_2, got_1, got_2, xs, wts, bias)


def solution(mesh):
    grid = P("lat", "lon")
    in_specs = (P(None, "lat", "lon"),) + (grid,) * 5 + (P(),) * 6
    return jax.shard_map(local, mesh=mesh, in_specs=in_specs, out_specs=P(None, "lat", "lon"), check_vma=False)
```

```python
import jax
import jax.numpy as jnp
from jax import lax
from jax.experimental import pallas as pl
from jax.experimental.pallas import tpu as pltpu
from jax.sharding import PartitionSpec as P

BF = jnp.bfloat16
F32 = jnp.float32
MIB = 1024 * 1024

C = 64
CP = 32
R = 16
W = 1280
LT = 128
WX = W + LT
PEERS = 16
HELD = 4
SUBS = 4
SLOTS = 4
KINDS = 4
EDGE = 16
MSG = HELD * CP + EDGE
PAIRS = R // 2 - 1
TAP = 3 * (C + CP)
TAPS = 4 * TAP
TAPS_OUT = 12 * C
PARTS = 4


def vmem(n=1):
    return [pl.BlockSpec(memory_space=pltpu.VMEM)] * n


def smem(n=1):
    return [pl.BlockSpec(memory_space=pltpu.SMEM)] * n


def params(mib):
    return pltpu.CompilerParams(vmem_limit_bytes=mib * MIB)


def struct(shape, dtype=BF):
    return jax.ShapeDtypeStruct(shape, dtype)


def kept(shape, dtype=BF):
    return pltpu.VMEM(shape, dtype)


def hbm(n=1):
    return [pl.BlockSpec(memory_space=pltpu.HBM)] * n


def in_hbm(*arrays):
    return [pltpu.with_memory_space_constraint(a, pltpu.HBM) for a in arrays]


def in_vmem(*arrays):
    return [pltpu.with_memory_space_constraint(a, pltpu.VMEM) for a in arrays]


def iota(shape, dim):
    return lax.broadcasted_iota(jnp.int32, shape, dim)


def message_kernel(noisy, coarse_hbm, ids, out, tiles, coarse, owner, slot, weight, counts, sems):
    me = lax.axis_index("lon")
    loads = [
        load(noisy.at[:, :, 0:LT], tiles.at[0], sems.at[0]),
        load(noisy.at[:, :, W - LT : W], tiles.at[1], sems.at[1]),
        load(coarse_hbm, coarse, sems.at[2]),
    ]
    loads += [load(a, b, sems.at[3 + i]) for i, (a, b) in enumerate(zip(ids, (owner, slot, weight, counts)))]
    for copy in loads:
        copy.wait()
    lane = iota((C, R, LT), 2)
    edge = jnp.where(lane < 64, tiles[0].astype(F32), tiles[1].astype(F32))
    edge = jnp.swapaxes(edge.astype(BF), 0, 1)
    edge = jnp.concatenate([edge[r] for r in range(R)], axis=1)
    row = iota((R * LT, LT), 0)
    col = iota((R * LT, LT), 1)
    at = row % LT
    kind = jnp.where(at < 64, at, at - 124)
    wanted = ((at < 2) | (at >= 126)) & (col == kind * R + row // LT)
    pick = jnp.where(wanted, 1.0, 0.0).astype(BF)
    packed = jnp.dot(edge, pick, preferred_element_type=F32)
    sides = []
    for side in range(2):
        parts = [packed[g * EDGE : (g + 1) * EDGE, side * 32 : side * 32 + 32] for g in range(C // EDGE)]
        sides.append(jnp.concatenate(parts, axis=1))
    lanes = iota((2, HELD, LT), 2)
    lists = jnp.zeros((2, HELD, LT), F32)
    for s in range(SUBS):
        live = counts[0, 0, s]
        for k in range(SLOTS):
            n = s * SLOTS + k
            block = owner[0, 0, s, k] * HELD + slot[0, 0, s, k]
            kind_id = jnp.where(k < live, weight[0, 0, s, k], KINDS)
            lists = jnp.where(lanes == n, block.astype(F32), lists)
            lists = jnp.where(lanes == 16 + n, kind_id.astype(F32), lists)
    chans = coarse[0].astype(F32)
    blocks = jnp.swapaxes(jnp.concatenate([chans, lists], axis=0), 0, 1)
    blocks = blocks.reshape(HELD * CP, LT).astype(BF)
    right = lax.rem(me + 1, PEERS)
    for p in range(PEERS):
        out[p, 0 : HELD * CP] = blocks
        out[p, HELD * CP :] = jnp.where(right == p, sides[1], sides[0]).astype(BF)


def message(noisy, coarse, *ids):
    def kernel(noisy_ref, coarse_ref, owner, slot, weight, counts, *rest):
        message_kernel(noisy_ref, coarse_ref, (owner, slot, weight, counts), *rest)

    return pl.pallas_call(
        kernel,
        out_shape=kept((PEERS, MSG, LT)),
        in_specs=hbm(6),
        out_specs=vmem()[0],
        scratch_shapes=[pltpu.VMEM((2, C, R, LT), BF), pltpu.VMEM(coarse.shape, BF)]
        + [pltpu.SMEM(a.shape, jnp.int32) for a in ids]
        + [pltpu.SemaphoreType.DMA((7,))],
        compiler_params=params(12),
    )(*in_hbm(noisy, coarse, *ids))


def load(src, dst, sem):
    copy = pltpu.make_async_copy(src, dst, sem)
    copy.start()
    return copy


def shifted(x, width):
    return [pltpu.roll(x, 1, 1), x, pltpu.roll(x, width - 1, 1)]


def pair_weights(taps):
    rows = jnp.concatenate(taps, axis=1)
    blank = jnp.zeros((rows.shape[0], rows.shape[1] // 3), BF)
    return jnp.concatenate(
        [jnp.concatenate([rows, blank], axis=1), jnp.concatenate([blank, rows], axis=1)], axis=0
    )


def cond_tap(tap):
    tap = jnp.concatenate([tap.astype(F32), jnp.zeros((CP - tap.shape[0], tap.shape[1]), F32)], axis=0)
    return tap.T.astype(BF)


def bias_column(row):
    same = iota((C, C), 0) == iota((C, C), 1)
    column = jnp.sum(jnp.where(same, row, 0.0), axis=1, keepdims=True)
    return jnp.concatenate([column, column], axis=0)


def near_rows():
    odd = lax.rem(lax.axis_index("lat"), 2)
    return (1 - odd) * (R - 2), odd * (R - 2)


def turn_kernel(
    noisy, params_hbm, xs, first, second, wts_hbm, bias_hbm, buf, wts, bias, small, sems, small_sems
):
    small_loads = [load(a, b, small_sems.at[i]) for i, (a, b) in enumerate(zip(params_hbm, small))]
    conv_in, conv_cond, conv_out, bias_in, bias_out = small
    loads = []
    for g in range(PARTS):
        part = pl.ds(g * (C // PARTS), C // PARTS)
        loads.append(load(noisy.at[part], buf.at[part], sems.at[g]))
    for copy in small_loads:
        copy.wait()
    taps = []
    for i in range(3):
        taps += [conv_in[i, j] for j in range(3)] + [cond_tap(conv_cond[i, j]) for j in range(3)]
    wts[:, 0:TAPS] = pair_weights(taps)
    wts[:, TAPS:] = pair_weights([conv_out[i, j] for i in range(3) for j in range(3)])
    bias[:, 0:LT] = jnp.broadcast_to(bias_column(bias_in[...]), (2 * C, LT))
    bias[:, LT:] = jnp.broadcast_to(bias_column(bias_out[...]), (2 * C, LT))
    stores = [load(wts, wts_hbm, sems.at[PARTS]), load(bias, bias_hbm, sems.at[PARTS + 1])]
    for copy in loads:
        copy.wait()
    xs[...] = jnp.swapaxes(buf[...], 0, 1).reshape(R * C, W)
    for i, (out, r0) in enumerate(zip((first, second), near_rows())):
        rows = pl.ds(pl.multiple_of(r0 * C, C), 2 * C)
        stores.append(load(xs.at[rows], out, sems.at[PARTS + 2 + i]))
    for copy in stores:
        copy.wait()


def turned(noisy, *small):
    count = len(small)

    def kernel(noisy_ref, *refs):
        scratch = refs[count + 5 :]
        turn_kernel(
            noisy_ref, refs[:count], *refs[count : count + 5], *scratch[:3], scratch[3 : 3 + count], *scratch[3 + count :]
        )

    return pl.pallas_call(
        kernel,
        out_shape=(
            kept((R * C, W)),
            pltpu.HBM((2 * C, W), BF),
            pltpu.HBM((2 * C, W), BF),
            pltpu.HBM((2 * C, TAPS + TAPS_OUT), BF),
            pltpu.HBM((2 * C, 2 * LT), F32),
        ),
        in_specs=hbm(1 + count),
        out_specs=tuple(vmem(1) + hbm(4)),
        scratch_shapes=[
            pltpu.VMEM((C, R, W), BF),
            pltpu.VMEM((2 * C, TAPS + TAPS_OUT), BF),
            pltpu.VMEM((2 * C, 2 * LT), F32),
        ]
        + [pltpu.VMEM(a.shape, a.dtype) for a in small]
        + [pltpu.SemaphoreType.DMA((PARTS + 4,)), pltpu.SemaphoreType.DMA((count,))],
        compiler_params=params(10),
        cost_estimate=pl.CostEstimate(flops=3 * 10**9, bytes_accessed=12 * 10**6, transcendentals=0),
    )(*in_hbm(noisy, *small))


def cond_kernel(got, table_hbm, wts_hbm, bias_hbm, cond, halo, first, second, wts, bias, acc, grp, ints, lists, table, sem, sems):
    loads = []
    for r in range(R // SUBS):
        loads.append(load(table_hbm.at[:, pl.ds(r * W, W)], table.at[r], sems.at[r]))
    others = [load(wts_hbm, wts, sems.at[R // SUBS]), load(bias_hbm, bias, sems.at[R // SUBS + 1])]
    me = lax.axis_index("lon")
    left = lax.rem(me + PEERS - 1, PEERS)
    right = lax.rem(me + 1, PEERS)
    for d, p in enumerate((me, left, right)):
        ints[d] = got[p, CP - 16 : CP, :].astype(F32).astype(jnp.int32)
    copy = load(ints, lists, sem)
    acc[...] = jnp.zeros_like(acc)

    rows = []
    for g in range(C // EDGE):
        cols = slice(g * 32, g * 32 + 32)
        side = [got[p, HELD * CP :, cols].astype(F32) for p in (right, left)]
        rows.append(jnp.concatenate(side + [jnp.zeros((EDGE, 64), F32)], axis=1))
    both = jnp.concatenate(rows, axis=0).astype(BF)
    src = iota((LT, R * LT), 0)
    dst = iota((LT, R * LT), 1)
    at = dst % LT
    kind = jnp.where(at < 64, at, at - 124)
    wanted = ((at < 2) | (at >= 126)) & (src == kind * R + dst // LT)
    place = jnp.where(wanted, 1.0, 0.0).astype(BF)
    tiles = jnp.dot(both, place, preferred_element_type=F32).astype(BF)
    for r in range(R):
        halo[pl.ds(r * C, C), :] = tiles[:, r * LT : (r + 1) * LT]

    copy.wait()
    for d in range(3):
        for s in range(SUBS):
            for k in range(SLOTS):
                n = s * SLOTS + k
                block = lists[d, 14, n]
                part = got[block // HELD, pl.ds(pl.multiple_of(lax.rem(block, HELD) * CP, CP), CP), :]
                at = (d * SUBS + s) * (KINDS + 1) + lists[d, 14, 16 + n]
                acc[at] = acc[at] + part.astype(F32)
    for d in range(3):
        for s in range(SUBS):
            for w in range(KINDS):
                grp[d, pl.ds(s * CP, CP), w * LT : (w + 1) * LT] = acc[(d * SUBS + s) * (KINDS + 1) + w].astype(BF)

    lane = iota((SUBS * CP, LT), 1)
    for r in range(R // SUBS):
        if r % 2 == 0:
            loads[r].wait()
            loads[r + 1].wait()
        part = table.at[r]
        own = jnp.dot(grp[0], part[...], preferred_element_type=F32).astype(BF)
        lhs = jnp.dot(grp[1], part[:, W - LT : W], preferred_element_type=F32)
        rhs = jnp.dot(grp[2], part[:, 0:LT], preferred_element_type=F32)
        side = jnp.where(lane < 2, rhs, jnp.where(lane >= 126, lhs, 0.0)).astype(BF)
        for s in range(SUBS):
            at = pl.ds((s * SUBS + r) * CP, CP)
            cond[at, 0:W] = own[s * CP : (s + 1) * CP]
            cond[at, W:WX] = side[s * CP : (s + 1) * CP]
    for out, r0 in zip((first, second), near_rows()):
        out[:, 0:WX] = cond[pl.ds(pl.multiple_of(r0 * CP, CP), 2 * CP), :]
        for j in range(2):
            out[:, WX + j * LT : WX + (j + 1) * LT] = halo[pl.ds(pl.multiple_of((r0 + j) * C, C), C), :]
    for copy in others:
        copy.wait()


def cond_tile(got, table, wts, bias):
    edge = struct((2 * CP, WX + 2 * LT))
    return pl.pallas_call(
        cond_kernel,
        out_shape=(
            kept((R * CP, WX)),
            kept((R * C, LT)),
            edge,
            edge,
            kept(wts.shape),
            kept(bias.shape, F32),
        ),
        in_specs=vmem(1) + hbm(3),
        out_specs=tuple(vmem(6)),
        scratch_shapes=[
            pltpu.VMEM((3 * SUBS * (KINDS + 1), CP, LT), F32),
            pltpu.VMEM((3, SUBS * CP, KINDS * LT), BF),
            pltpu.VMEM((3, 16, LT), jnp.int32),
            pltpu.SMEM((3, 16, LT), jnp.int32),
            pltpu.VMEM((R // SUBS, KINDS * LT, W), BF),
            pltpu.SemaphoreType.DMA,
            pltpu.SemaphoreType.DMA((R // SUBS + 2,)),
        ],
        compiler_params=params(14),
    )(*in_vmem(got), *in_hbm(table, wts, bias))


def silu(v):
    return v / (1.0 + jnp.exp(-v))


def put_taps(dst, row, noisy, cond):
    at = row * TAP
    for d, y in enumerate(shifted(noisy, WX)):
        dst[pl.ds(at + d * C, C), :] = y
    for d, y in enumerate(shifted(cond, WX)):
        dst[pl.ds(at + 3 * C + d * CP, CP), :] = y


def put_act(dst, row, x):
    for d, y in enumerate(shifted(x, WX)):
        dst[pl.ds((row * 3 + d) * C, C), :] = y[:, 0:W]


def own_row(xs, halo, r):
    return jnp.concatenate([xs[pl.ds(r * C, C), :], halo[pl.ds(r * C, C), :]], axis=1)


def first_conv(wts, bias, rows):
    return silu(jnp.dot(wts[:, 0:TAPS], rows, preferred_element_type=F32) + bias[:, 0:1])


def second_conv(wts, bias, rows, x):
    y = jnp.dot(wts[:, TAPS:], rows, preferred_element_type=F32)
    return (y + x.astype(F32) + bias[:, LT : LT + 1]).astype(BF)


def inner_kernel(cond, halo, xs, wts, bias, noisy_hbm, zi, edge, noisy_2, x3, a3, sem):
    near = load(noisy_hbm, noisy_2, sem)
    for r in range(R):
        put_taps(x3, r, own_row(xs, halo, r), cond[pl.ds(r * CP, CP), :])
    for i in range(PAIRS):
        a = first_conv(wts, bias, x3[pl.ds(2 * i * TAP, TAPS), :]).astype(BF)
        for j in range(2):
            r = i * 2 + j
            x = a[j * C : (j + 1) * C]
            if r < 2 or r >= R - 4:
                edge[pl.ds((r if r < 2 else r - R + 6) * C, C), :] = x
            put_act(a3, r, x)
    for i in range(PAIRS - 1):
        x = xs[pl.ds((i + 1) * 2 * C, 2 * C), :]
        zi[pl.ds(i * 2 * C, 2 * C), :] = second_conv(wts, bias, a3[pl.ds(i * 6 * C, TAPS_OUT), :], x)
    near.wait()


def inner_rows(cond, halo, xs, wts, bias, noisy_2):
    return pl.pallas_call(
        inner_kernel,
        out_shape=(kept(((R - 4) * C, W)), kept((4 * C, WX)), kept((2 * C, W))),
        in_specs=vmem(5) + hbm(1),
        out_specs=tuple(vmem(3)),
        scratch_shapes=[
            pltpu.VMEM((R * TAP, WX), BF),
            pltpu.VMEM(((R - 2) * 3 * C, W), BF),
            pltpu.SemaphoreType.DMA,
        ],
        compiler_params=params(26),
        cost_estimate=pl.CostEstimate(flops=6 * 10**9, bytes_accessed=12 * 10**6, transcendentals=10**6),
    )(*in_vmem(cond, halo, xs, wts, bias), *in_hbm(noisy_2))


def outer_kernel(
    zi, edge, cond, halo, noisy_1, noisy_2, got_1, got_2, xs, wts, bias, out, x3, a3, buf, sems
):
    lat = lax.axis_index("lat")
    half = R // 2
    each = C // PARTS
    upper = jnp.where(lat == 0, 0.0, 1.0)
    lower = jnp.where(lat == lax.axis_size("lat") - 1, 0.0, 1.0)

    def both_sides(odd):
        copies = []
        sides = ((1 - odd, got_1), (odd, got_2))
        for k, (low, _) in enumerate(sides):
            for j in range(2):
                put_act(a3.at[k], (1 - low) * 2 + j, edge[pl.ds((low * 2 + j) * C, C), :])
                r = low * (R - 2) + j
                put_taps(x3.at[k], (1 - low) * 2 + j, own_row(xs, halo, r), cond[pl.ds(r * CP, CP), :])
        for k, (low, got) in enumerate(sides):
            noisy = noisy_2 if k else noisy_1
            for j in range(2):
                tile = got[:, WX + j * LT : WX + (j + 1) * LT]
                x = jnp.concatenate([noisy[pl.ds(j * C, C), :], tile], axis=1)
                put_taps(x3.at[k], low * 2 + j, x, got[j * CP : (j + 1) * CP, 0:WX])
            v = first_conv(wts, bias, x3[k])
            v0, v1 = (v[0:C], v[C:] * lower) if low else (v[0:C] * upper, v[C:])
            put_act(a3.at[k], low * 2, v0.astype(BF))
            put_act(a3.at[k], low * 2 + 1, v1.astype(BF))
            z = second_conv(wts, bias, a3[k], xs[pl.ds(low * (R - 2) * C, 2 * C), :])
            rows = [z[0:C], z[C:]]
            inner = [zi[pl.ds((low * (half - 2) + r) * C, C), :] for r in range(half - 2)]
            rows = inner + rows if low else rows + inner
            here = pl.ds(low * half, half)
            for g in range(PARTS):
                chans = pl.ds(g * each, each)
                group = jnp.stack([row[g * each : (g + 1) * each] for row in rows], axis=0)
                buf[k, chans] = jnp.swapaxes(group, 0, 1)
                copies.append(load(buf.at[k, chans], out.at[chans, here, :], sems.at[k * PARTS + g]))
        for copy in copies:
            copy.wait()

    for odd in range(2):
        pl.when(lax.rem(lat, 2) == odd)(lambda odd=odd: both_sides(odd))


def outer_rows(zi, edge, cond, halo, noisy_1, noisy_2, got_1, got_2, xs, wts, bias):
    return pl.pallas_call(
        outer_kernel,
        out_shape=pltpu.HBM((C, R, W), BF),
        in_specs=vmem(11),
        out_specs=hbm(1)[0],
        scratch_shapes=[
            pltpu.VMEM((2, TAPS, WX), BF),
            pltpu.VMEM((2, TAPS_OUT, W), BF),
            pltpu.VMEM((2, C, R // 2, W), BF),
            pltpu.SemaphoreType.DMA((2 * PARTS,)),
        ],
        compiler_params=params(24),
    )(*in_vmem(zi, edge, cond, halo), noisy_1, *in_vmem(noisy_2), got_1, got_2, *in_vmem(xs, wts, bias))


def exchanged(first, second):
    count = lax.axis_size("lat")
    got_1 = lax.ppermute(first, "lat", [(i, i ^ 1) for i in range(count)])
    got_2 = lax.ppermute(second, "lat", [(i, ((i + 1) ^ 1) - 1) for i in range(1, count - 1)])
    return got_1, got_2


def local(noisy, coarse, owner, slot, weight, counts, table, conv_in, conv_cond, bias_in, conv_out, bias_out):
    coarse = jnp.transpose(coarse, (0, 2, 1, 3))
    conv_cond = jnp.transpose(conv_cond, (0, 1, 3, 2))
    table = table.reshape(KINDS * LT, table.shape[2])
    msg = message(noisy, coarse, owner, slot, weight, counts)
    got = lax.all_to_all(msg, "lon", split_axis=0, concat_axis=0, tiled=True)
    xs, first, second, wts, bias = turned(noisy, conv_in, conv_cond, conv_out, bias_in[None], bias_out[None])
    noisy_1, noisy_2 = exchanged(first, second)
    cond, halo, first, second, wts, bias = cond_tile(got, table, wts, bias)
    got_1, got_2 = exchanged(first, second)
    zi, edge, noisy_2 = inner_rows(cond, halo, xs, wts, bias, noisy_2)
    return outer_rows(zi, edge, cond, halo, noisy_1, noisy_2, got_1, got_2, xs, wts, bias)


def solution(mesh):
    grid = P("lat", "lon")
    in_specs = (P(None, "lat", "lon"),) + (grid,) * 5 + (P(),) * 6
    return jax.shard_map(local, mesh=mesh, in_specs=in_specs, out_specs=P(None, "lat", "lon"), check_vma=False)
```

```python
import jax
import jax.numpy as jnp
from jax import lax
from jax.experimental import pallas as pl
from jax.experimental.pallas import tpu as pltpu
from jax.sharding import PartitionSpec as P

BF = jnp.bfloat16
F32 = jnp.float32
MIB = 1024 * 1024

C = 64
CP = 32
R = 16
W = 1280
LT = 128
WX = W + LT
PEERS = 16
HELD = 4
SUBS = 4
SLOTS = 4
KINDS = 4
EDGE = 16
MSG = HELD * CP + EDGE
PAIRS = R // 2 - 1
TAP = 3 * (C + CP)
TAPS = 4 * TAP
TAPS_OUT = 12 * C
PARTS = 4


def vmem(n=1):
    return [pl.BlockSpec(memory_space=pltpu.VMEM)] * n


def smem(n=1):
    return [pl.BlockSpec(memory_space=pltpu.SMEM)] * n


def params(mib):
    return pltpu.CompilerParams(vmem_limit_bytes=mib * MIB)


def struct(shape, dtype=BF):
    return jax.ShapeDtypeStruct(shape, dtype)


def kept(shape, dtype=BF):
    return pltpu.VMEM(shape, dtype)


def hbm(n=1):
    return [pl.BlockSpec(memory_space=pltpu.HBM)] * n


def in_hbm(*arrays):
    return [pltpu.with_memory_space_constraint(a, pltpu.HBM) for a in arrays]


def in_vmem(*arrays):
    return [pltpu.with_memory_space_constraint(a, pltpu.VMEM) for a in arrays]


def iota(shape, dim):
    return lax.broadcasted_iota(jnp.int32, shape, dim)


def message_kernel(noisy, coarse_hbm, ids, out, tiles, coarse, owner, slot, weight, counts, sems):
    me = lax.axis_index("lon")
    loads = [
        load(noisy.at[:, :, 0:LT], tiles.at[0], sems.at[0]),
        load(noisy.at[:, :, W - LT : W], tiles.at[1], sems.at[1]),
        load(coarse_hbm, coarse, sems.at[2]),
    ]
    loads += [load(a, b, sems.at[3 + i]) for i, (a, b) in enumerate(zip(ids, (owner, slot, weight, counts)))]
    for copy in loads:
        copy.wait()
    lane = iota((C, R, LT), 2)
    edge = jnp.where(lane < 64, tiles[0].astype(F32), tiles[1].astype(F32))
    edge = jnp.swapaxes(edge.astype(BF), 0, 1)
    edge = jnp.concatenate([edge[r] for r in range(R)], axis=1)
    row = iota((R * LT, LT), 0)
    col = iota((R * LT, LT), 1)
    at = row % LT
    kind = jnp.where(at < 64, at, at - 124)
    wanted = ((at < 2) | (at >= 126)) & (col == kind * R + row // LT)
    pick = jnp.where(wanted, 1.0, 0.0).astype(BF)
    packed = jnp.dot(edge, pick, preferred_element_type=F32)
    sides = []
    for side in range(2):
        parts = [packed[g * EDGE : (g + 1) * EDGE, side * 32 : side * 32 + 32] for g in range(C // EDGE)]
        sides.append(jnp.concatenate(parts, axis=1))
    lanes = iota((2, HELD, LT), 2)
    lists = jnp.zeros((2, HELD, LT), F32)
    for s in range(SUBS):
        live = counts[0, 0, s]
        for k in range(SLOTS):
            n = s * SLOTS + k
            block = owner[0, 0, s, k] * HELD + slot[0, 0, s, k]
            kind_id = jnp.where(k < live, weight[0, 0, s, k], KINDS)
            lists = jnp.where(lanes == n, block.astype(F32), lists)
            lists = jnp.where(lanes == 16 + n, kind_id.astype(F32), lists)
    chans = coarse[0].astype(F32)
    blocks = jnp.swapaxes(jnp.concatenate([chans, lists], axis=0), 0, 1)
    blocks = blocks.reshape(HELD * CP, LT).astype(BF)
    right = lax.rem(me + 1, PEERS)
    for p in range(PEERS):
        out[p, 0 : HELD * CP] = blocks
        out[p, HELD * CP :] = jnp.where(right == p, sides[1], sides[0]).astype(BF)


def message(noisy, coarse, *ids):
    def kernel(noisy_ref, coarse_ref, owner, slot, weight, counts, *rest):
        message_kernel(noisy_ref, coarse_ref, (owner, slot, weight, counts), *rest)

    return pl.pallas_call(
        kernel,
        out_shape=kept((PEERS, MSG, LT)),
        in_specs=hbm(6),
        out_specs=vmem()[0],
        scratch_shapes=[pltpu.VMEM((2, C, R, LT), BF), pltpu.VMEM(coarse.shape, BF)]
        + [pltpu.SMEM(a.shape, jnp.int32) for a in ids]
        + [pltpu.SemaphoreType.DMA((7,))],
        compiler_params=params(12),
    )(*in_hbm(noisy, coarse, *ids))


def load(src, dst, sem):
    copy = pltpu.make_async_copy(src, dst, sem)
    copy.start()
    return copy


def shifted(x, width):
    return [pltpu.roll(x, 1, 1), x, pltpu.roll(x, width - 1, 1)]


def pair_weights(taps):
    rows = jnp.concatenate(taps, axis=1)
    blank = jnp.zeros((rows.shape[0], rows.shape[1] // 3), BF)
    return jnp.concatenate(
        [jnp.concatenate([rows, blank], axis=1), jnp.concatenate([blank, rows], axis=1)], axis=0
    )


def cond_tap(tap):
    tap = jnp.concatenate([tap.astype(F32), jnp.zeros((CP - tap.shape[0], tap.shape[1]), F32)], axis=0)
    return tap.T.astype(BF)


def bias_column(row):
    same = iota((C, C), 0) == iota((C, C), 1)
    column = jnp.sum(jnp.where(same, row, 0.0), axis=1, keepdims=True)
    return jnp.concatenate([column, column], axis=0)


def near_rows():
    odd = lax.rem(lax.axis_index("lat"), 2)
    return (1 - odd) * (R - 2), odd * (R - 2)


def turn_kernel(
    noisy, params_hbm, xs, first, second, wts_hbm, bias_hbm, buf, wts, bias, small, sems, small_sems
):
    small_loads = [load(a, b, small_sems.at[i]) for i, (a, b) in enumerate(zip(params_hbm, small))]
    conv_in, conv_cond, conv_out, bias_in, bias_out = small
    loads = []
    for g in range(PARTS):
        part = pl.ds(g * (C // PARTS), C // PARTS)
        loads.append(load(noisy.at[part], buf.at[part], sems.at[g]))
    for copy in small_loads:
        copy.wait()
    taps = []
    for i in range(3):
        taps += [conv_in[i, j] for j in range(3)] + [cond_tap(conv_cond[i, j]) for j in range(3)]
    wts[:, 0:TAPS] = pair_weights(taps)
    wts[:, TAPS:] = pair_weights([conv_out[i, j] for i in range(3) for j in range(3)])
    bias[:, 0:LT] = jnp.broadcast_to(bias_column(bias_in[...]), (2 * C, LT))
    bias[:, LT:] = jnp.broadcast_to(bias_column(bias_out[...]), (2 * C, LT))
    stores = [load(wts, wts_hbm, sems.at[PARTS]), load(bias, bias_hbm, sems.at[PARTS + 1])]
    for copy in loads:
        copy.wait()
    xs[...] = jnp.swapaxes(buf[...], 0, 1).reshape(R * C, W)
    for i, (out, r0) in enumerate(zip((first, second), near_rows())):
        rows = pl.ds(pl.multiple_of(r0 * C, C), 2 * C)
        stores.append(load(xs.at[rows], out, sems.at[PARTS + 2 + i]))
    for copy in stores:
        copy.wait()


def turned(noisy, *small):
    count = len(small)

    def kernel(noisy_ref, *refs):
        scratch = refs[count + 5 :]
        turn_kernel(
            noisy_ref, refs[:count], *refs[count : count + 5], *scratch[:3], scratch[3 : 3 + count], *scratch[3 + count :]
        )

    return pl.pallas_call(
        kernel,
        out_shape=(
            kept((R * C, W)),
            pltpu.HBM((2 * C, W), BF),
            pltpu.HBM((2 * C, W), BF),
            pltpu.HBM((2 * C, TAPS + TAPS_OUT), BF),
            pltpu.HBM((2 * C, 2 * LT), F32),
        ),
        in_specs=hbm(1 + count),
        out_specs=tuple(vmem(1) + hbm(4)),
        scratch_shapes=[
            pltpu.VMEM((C, R, W), BF),
            pltpu.VMEM((2 * C, TAPS + TAPS_OUT), BF),
            pltpu.VMEM((2 * C, 2 * LT), F32),
        ]
        + [pltpu.VMEM(a.shape, a.dtype) for a in small]
        + [pltpu.SemaphoreType.DMA((PARTS + 4,)), pltpu.SemaphoreType.DMA((count,))],
        compiler_params=params(10),
        cost_estimate=pl.CostEstimate(flops=3 * 10**9, bytes_accessed=12 * 10**6, transcendentals=0),
    )(*in_hbm(noisy, *small))


def cond_kernel(got, table_hbm, wts_hbm, bias_hbm, cond, halo, first, second, wts, bias, acc, grp, ints, lists, table, sem, sems):
    loads = []
    for r in range(R // SUBS):
        loads.append(load(table_hbm.at[:, pl.ds(r * W, W)], table.at[r], sems.at[r]))
    others = [load(wts_hbm, wts, sems.at[R // SUBS]), load(bias_hbm, bias, sems.at[R // SUBS + 1])]
    me = lax.axis_index("lon")
    left = lax.rem(me + PEERS - 1, PEERS)
    right = lax.rem(me + 1, PEERS)
    for d, p in enumerate((me, left, right)):
        ints[d] = got[p, CP - 16 : CP, :].astype(F32).astype(jnp.int32)
    copy = load(ints, lists, sem)
    acc[...] = jnp.zeros_like(acc)

    rows = []
    for g in range(C // EDGE):
        cols = slice(g * 32, g * 32 + 32)
        side = [got[p, HELD * CP :, cols].astype(F32) for p in (right, left)]
        rows.append(jnp.concatenate(side + [jnp.zeros((EDGE, 64), F32)], axis=1))
    both = jnp.concatenate(rows, axis=0).astype(BF)
    src = iota((LT, R * LT), 0)
    dst = iota((LT, R * LT), 1)
    at = dst % LT
    kind = jnp.where(at < 64, at, at - 124)
    wanted = ((at < 2) | (at >= 126)) & (src == kind * R + dst // LT)
    place = jnp.where(wanted, 1.0, 0.0).astype(BF)
    tiles = jnp.dot(both, place, preferred_element_type=F32).astype(BF)
    for r in range(R):
        halo[pl.ds(r * C, C), :] = tiles[:, r * LT : (r + 1) * LT]

    copy.wait()
    for d in range(3):
        for s in range(SUBS):
            for k in range(SLOTS):
                n = s * SLOTS + k
                block = lists[d, 14, n]
                part = got[block // HELD, pl.ds(pl.multiple_of(lax.rem(block, HELD) * CP, CP), CP), :]
                at = (d * SUBS + s) * (KINDS + 1) + lists[d, 14, 16 + n]
                acc[at] = acc[at] + part.astype(F32)
    for d in range(3):
        for s in range(SUBS):
            for w in range(KINDS):
                grp[d, pl.ds(s * CP, CP), w * LT : (w + 1) * LT] = acc[(d * SUBS + s) * (KINDS + 1) + w].astype(BF)

    lane = iota((SUBS * CP, LT), 1)
    for r in range(R // SUBS):
        if r % 2 == 0:
            loads[r].wait()
            loads[r + 1].wait()
            lt = jnp.concatenate([table[q, :, W - LT : W] for q in (r, r + 1)], axis=1)
            rt = jnp.concatenate([table[q, :, 0:LT] for q in (r, r + 1)], axis=1)
            lhs_2 = jnp.dot(grp[1], lt, preferred_element_type=F32)
            rhs_2 = jnp.dot(grp[2], rt, preferred_element_type=F32)
        part = table.at[r]
        tile = slice(r % 2 * LT, (r % 2 + 1) * LT)
        own = jnp.dot(grp[0], part[...], preferred_element_type=F32).astype(BF)
        lhs, rhs = lhs_2[:, tile], rhs_2[:, tile]
        side = jnp.where(lane < 2, rhs, jnp.where(lane >= 126, lhs, 0.0)).astype(BF)
        for s in range(SUBS):
            at = pl.ds((s * SUBS + r) * CP, CP)
            cond[at, 0:W] = own[s * CP : (s + 1) * CP]
            cond[at, W:WX] = side[s * CP : (s + 1) * CP]
    for out, r0 in zip((first, second), near_rows()):
        out[:, 0:WX] = cond[pl.ds(pl.multiple_of(r0 * CP, CP), 2 * CP), :]
        for j in range(2):
            out[:, WX + j * LT : WX + (j + 1) * LT] = halo[pl.ds(pl.multiple_of((r0 + j) * C, C), C), :]
    for copy in others:
        copy.wait()


def cond_tile(got, table, wts, bias):
    edge = struct((2 * CP, WX + 2 * LT))
    return pl.pallas_call(
        cond_kernel,
        out_shape=(
            kept((R * CP, WX)),
            kept((R * C, LT)),
            edge,
            edge,
            kept(wts.shape),
            kept(bias.shape, F32),
        ),
        in_specs=vmem(1) + hbm(3),
        out_specs=tuple(vmem(6)),
        scratch_shapes=[
            pltpu.VMEM((3 * SUBS * (KINDS + 1), CP, LT), F32),
            pltpu.VMEM((3, SUBS * CP, KINDS * LT), BF),
            pltpu.VMEM((3, 16, LT), jnp.int32),
            pltpu.SMEM((3, 16, LT), jnp.int32),
            pltpu.VMEM((R // SUBS, KINDS * LT, W), BF),
            pltpu.SemaphoreType.DMA,
            pltpu.SemaphoreType.DMA((R // SUBS + 2,)),
        ],
        compiler_params=params(14),
    )(*in_vmem(got), *in_hbm(table, wts, bias))


def silu(v):
    return v / (1.0 + jnp.exp(-v))


def put_taps(dst, row, noisy, cond):
    at = row * TAP
    for d, y in enumerate(shifted(noisy, WX)):
        dst[pl.ds(at + d * C, C), :] = y
    for d, y in enumerate(shifted(cond, WX)):
        dst[pl.ds(at + 3 * C + d * CP, CP), :] = y


def put_act(dst, row, x):
    for d, y in enumerate(shifted(x, WX)):
        dst[pl.ds((row * 3 + d) * C, C), :] = y[:, 0:W]


def own_row(xs, halo, r):
    return jnp.concatenate([xs[pl.ds(r * C, C), :], halo[pl.ds(r * C, C), :]], axis=1)


def first_conv(wts, bias, rows):
    return silu(jnp.dot(wts[:, 0:TAPS], rows, preferred_element_type=F32) + bias[:, 0:1])


def second_conv(wts, bias, rows, x):
    y = jnp.dot(wts[:, TAPS:], rows, preferred_element_type=F32)
    return (y + x.astype(F32) + bias[:, LT : LT + 1]).astype(BF)


def inner_kernel(cond, halo, xs, wts, bias, noisy_hbm, zi, edge, noisy_2, x3, a3, sem):
    near = load(noisy_hbm, noisy_2, sem)
    for r in range(R):
        put_taps(x3, r, own_row(xs, halo, r), cond[pl.ds(r * CP, CP), :])
    for i in range(PAIRS):
        a = first_conv(wts, bias, x3[pl.ds(2 * i * TAP, TAPS), :]).astype(BF)
        for j in range(2):
            r = i * 2 + j
            x = a[j * C : (j + 1) * C]
            if r < 2 or r >= R - 4:
                edge[pl.ds((r if r < 2 else r - R + 6) * C, C), :] = x
            put_act(a3, r, x)
    for i in range(PAIRS - 1):
        x = xs[pl.ds((i + 1) * 2 * C, 2 * C), :]
        zi[pl.ds(i * 2 * C, 2 * C), :] = second_conv(wts, bias, a3[pl.ds(i * 6 * C, TAPS_OUT), :], x)
    near.wait()


def inner_rows(cond, halo, xs, wts, bias, noisy_2):
    return pl.pallas_call(
        inner_kernel,
        out_shape=(kept(((R - 4) * C, W)), kept((4 * C, WX)), kept((2 * C, W))),
        in_specs=vmem(5) + hbm(1),
        out_specs=tuple(vmem(3)),
        scratch_shapes=[
            pltpu.VMEM((R * TAP, WX), BF),
            pltpu.VMEM(((R - 2) * 3 * C, W), BF),
            pltpu.SemaphoreType.DMA,
        ],
        compiler_params=params(26),
        cost_estimate=pl.CostEstimate(flops=6 * 10**9, bytes_accessed=12 * 10**6, transcendentals=10**6),
    )(*in_vmem(cond, halo, xs, wts, bias), *in_hbm(noisy_2))


def outer_kernel(
    zi, edge, cond, halo, noisy_1, noisy_2, got_1, got_2, xs, wts, bias, out, x3, a3, buf, sems
):
    lat = lax.axis_index("lat")
    each = C // PARTS
    upper = jnp.where(lat == 0, 0.0, 1.0)
    lower = jnp.where(lat == lax.axis_size("lat") - 1, 0.0, 1.0)

    def both_sides(odd):
        copies = []
        ends = {}
        sides = ((1 - odd, got_1), (odd, got_2))
        for k, (low, _) in enumerate(sides):
            for j in range(2):
                put_act(a3.at[k], (1 - low) * 2 + j, edge[pl.ds((low * 2 + j) * C, C), :])
                r = low * (R - 2) + j
                put_taps(x3.at[k], (1 - low) * 2 + j, own_row(xs, halo, r), cond[pl.ds(r * CP, CP), :])
        for k, (low, got) in enumerate(sides):
            noisy = noisy_2 if k else noisy_1
            for j in range(2):
                tile = got[:, WX + j * LT : WX + (j + 1) * LT]
                x = jnp.concatenate([noisy[pl.ds(j * C, C), :], tile], axis=1)
                put_taps(x3.at[k], low * 2 + j, x, got[j * CP : (j + 1) * CP, 0:WX])
            v = first_conv(wts, bias, x3[k])
            v0, v1 = (v[0:C], v[C:] * lower) if low else (v[0:C] * upper, v[C:])
            put_act(a3.at[k], low * 2, v0.astype(BF))
            put_act(a3.at[k], low * 2 + 1, v1.astype(BF))
            z = second_conv(wts, bias, a3[k], xs[pl.ds(low * (R - 2) * C, 2 * C), :])
            ends[low] = [z[0:C], z[C:]]
        rows = ends[0] + [zi[pl.ds(r * C, C), :] for r in range(R - 4)] + ends[1]
        for g in range(PARTS):
            chans = pl.ds(g * each, each)
            group = jnp.stack([row[g * each : (g + 1) * each] for row in rows], axis=0)
            buf[chans] = jnp.swapaxes(group, 0, 1)
            copies.append(load(buf.at[chans], out.at[chans], sems.at[g]))
        for copy in copies:
            copy.wait()

    for odd in range(2):
        pl.when(lax.rem(lat, 2) == odd)(lambda odd=odd: both_sides(odd))


def outer_rows(zi, edge, cond, halo, noisy_1, noisy_2, got_1, got_2, xs, wts, bias):
    return pl.pallas_call(
        outer_kernel,
        out_shape=pltpu.HBM((C, R, W), BF),
        in_specs=vmem(11),
        out_specs=hbm(1)[0],
        scratch_shapes=[
            pltpu.VMEM((2, TAPS, WX), BF),
            pltpu.VMEM((2, TAPS_OUT, W), BF),
            pltpu.VMEM((C, R, W), BF),
            pltpu.SemaphoreType.DMA((PARTS,)),
        ],
        compiler_params=params(24),
    )(*in_vmem(zi, edge, cond, halo), noisy_1, *in_vmem(noisy_2), got_1, got_2, *in_vmem(xs, wts, bias))


def exchanged(first, second):
    count = lax.axis_size("lat")
    got_1 = lax.ppermute(first, "lat", [(i, i ^ 1) for i in range(count)])
    got_2 = lax.ppermute(second, "lat", [(i, ((i + 1) ^ 1) - 1) for i in range(1, count - 1)])
    return got_1, got_2


def local(noisy, coarse, owner, slot, weight, counts, table, conv_in, conv_cond, bias_in, conv_out, bias_out):
    coarse = jnp.transpose(coarse, (0, 2, 1, 3))
    conv_cond = jnp.transpose(conv_cond, (0, 1, 3, 2))
    table = table.reshape(KINDS * LT, table.shape[2])
    msg = message(noisy, coarse, owner, slot, weight, counts)
    got = lax.all_to_all(msg, "lon", split_axis=0, concat_axis=0, tiled=True)
    xs, first, second, wts, bias = turned(noisy, conv_in, conv_cond, conv_out, bias_in[None], bias_out[None])
    noisy_1, noisy_2 = exchanged(first, second)
    cond, halo, first, second, wts, bias = cond_tile(got, table, wts, bias)
    got_1, got_2 = exchanged(first, second)
    zi, edge, noisy_2 = inner_rows(cond, halo, xs, wts, bias, noisy_2)
    return outer_rows(zi, edge, cond, halo, noisy_1, noisy_2, got_1, got_2, xs, wts, bias)


def solution(mesh):
    grid = P("lat", "lon")
    in_specs = (P(None, "lat", "lon"),) + (grid,) * 5 + (P(),) * 6
    return jax.shard_map(local, mesh=mesh, in_specs=in_specs, out_specs=P(None, "lat", "lon"), check_vma=False)
```

```python
import jax
import jax.numpy as jnp
from jax import lax
from jax.experimental import pallas as pl
from jax.experimental.pallas import tpu as pltpu
from jax.sharding import PartitionSpec as P

BF = jnp.bfloat16
F32 = jnp.float32
MIB = 1024 * 1024

C = 64
CP = 32
R = 16
W = 1280
LT = 128
WX = W + LT
PEERS = 16
HELD = 4
SUBS = 4
SLOTS = 4
KINDS = 4
EDGE = 16
MSG = HELD * CP + EDGE
PAIRS = R // 2 - 1
TAP = 3 * (C + CP)
TAPS = 4 * TAP
TAPS_OUT = 12 * C
PARTS = 4


def vmem(n=1):
    return [pl.BlockSpec(memory_space=pltpu.VMEM)] * n


def smem(n=1):
    return [pl.BlockSpec(memory_space=pltpu.SMEM)] * n


def params(mib):
    return pltpu.CompilerParams(vmem_limit_bytes=mib * MIB)


def struct(shape, dtype=BF):
    return jax.ShapeDtypeStruct(shape, dtype)


def kept(shape, dtype=BF):
    return pltpu.VMEM(shape, dtype)


def hbm(n=1):
    return [pl.BlockSpec(memory_space=pltpu.HBM)] * n


def in_hbm(*arrays):
    return [pltpu.with_memory_space_constraint(a, pltpu.HBM) for a in arrays]


def in_vmem(*arrays):
    return [pltpu.with_memory_space_constraint(a, pltpu.VMEM) for a in arrays]


def iota(shape, dim):
    return lax.broadcasted_iota(jnp.int32, shape, dim)


def message_kernel(noisy, coarse_hbm, ids, out, tiles, coarse, owner, slot, weight, counts, sems):
    me = lax.axis_index("lon")
    loads = [
        load(noisy.at[:, :, 0:LT], tiles.at[0], sems.at[0]),
        load(noisy.at[:, :, W - LT : W], tiles.at[1], sems.at[1]),
        load(coarse_hbm, coarse, sems.at[2]),
    ]
    loads += [load(a, b, sems.at[3 + i]) for i, (a, b) in enumerate(zip(ids, (owner, slot, weight, counts)))]
    for copy in loads:
        copy.wait()
    lane = iota((C, R, LT), 2)
    edge = jnp.where(lane < 64, tiles[0].astype(F32), tiles[1].astype(F32))
    edge = jnp.swapaxes(edge.astype(BF), 0, 1)
    edge = jnp.concatenate([edge[r] for r in range(R)], axis=1)
    row = iota((R * LT, LT), 0)
    col = iota((R * LT, LT), 1)
    at = row % LT
    kind = jnp.where(at < 64, at, at - 124)
    wanted = ((at < 2) | (at >= 126)) & (col == kind * R + row // LT)
    pick = jnp.where(wanted, 1.0, 0.0).astype(BF)
    packed = jnp.dot(edge, pick, preferred_element_type=F32)
    sides = []
    for side in range(2):
        parts = [packed[g * EDGE : (g + 1) * EDGE, side * 32 : side * 32 + 32] for g in range(C // EDGE)]
        sides.append(jnp.concatenate(parts, axis=1))
    lanes = iota((2, HELD, LT), 2)
    lists = jnp.zeros((2, HELD, LT), F32)
    for s in range(SUBS):
        live = counts[0, 0, s]
        for k in range(SLOTS):
            n = s * SLOTS + k
            block = owner[0, 0, s, k] * HELD + slot[0, 0, s, k]
            kind_id = jnp.where(k < live, weight[0, 0, s, k], KINDS)
            lists = jnp.where(lanes == n, block.astype(F32), lists)
            lists = jnp.where(lanes == 16 + n, kind_id.astype(F32), lists)
    chans = coarse[0].astype(F32)
    blocks = jnp.swapaxes(jnp.concatenate([chans, lists], axis=0), 0, 1)
    blocks = blocks.reshape(HELD * CP, LT).astype(BF)
    right = lax.rem(me + 1, PEERS)
    for p in range(PEERS):
        out[p, 0 : HELD * CP] = blocks
        out[p, HELD * CP :] = jnp.where(right == p, sides[1], sides[0]).astype(BF)


def message(noisy, coarse, *ids):
    def kernel(noisy_ref, coarse_ref, owner, slot, weight, counts, *rest):
        message_kernel(noisy_ref, coarse_ref, (owner, slot, weight, counts), *rest)

    return pl.pallas_call(
        kernel,
        out_shape=kept((PEERS, MSG, LT)),
        in_specs=hbm(6),
        out_specs=vmem()[0],
        scratch_shapes=[pltpu.VMEM((2, C, R, LT), BF), pltpu.VMEM(coarse.shape, BF)]
        + [pltpu.SMEM(a.shape, jnp.int32) for a in ids]
        + [pltpu.SemaphoreType.DMA((7,))],
        compiler_params=params(12),
    )(*in_hbm(noisy, coarse, *ids))


def load(src, dst, sem):
    copy = pltpu.make_async_copy(src, dst, sem)
    copy.start()
    return copy


def shifted(x, width):
    return [pltpu.roll(x, 1, 1), x, pltpu.roll(x, width - 1, 1)]


def pair_weights(taps):
    rows = jnp.concatenate(taps, axis=1)
    blank = jnp.zeros((rows.shape[0], rows.shape[1] // 3), BF)
    return jnp.concatenate(
        [jnp.concatenate([rows, blank], axis=1), jnp.concatenate([blank, rows], axis=1)], axis=0
    )


def cond_tap(tap):
    tap = jnp.concatenate([tap.astype(F32), jnp.zeros((CP - tap.shape[0], tap.shape[1]), F32)], axis=0)
    return tap.T.astype(BF)


def bias_column(row):
    same = iota((C, C), 0) == iota((C, C), 1)
    column = jnp.sum(jnp.where(same, row, 0.0), axis=1, keepdims=True)
    return jnp.concatenate([column, column], axis=0)


def near_rows():
    odd = lax.rem(lax.axis_index("lat"), 2)
    return (1 - odd) * (R - 2), odd * (R - 2)


def turn_kernel(
    noisy, params_hbm, xs, first, second, wts_hbm, bias_hbm, buf, wts, bias, small, sems, small_sems
):
    small_loads = [load(a, b, small_sems.at[i]) for i, (a, b) in enumerate(zip(params_hbm, small))]
    conv_in, conv_cond, conv_out, bias_in, bias_out = small
    loads = []
    for g in range(PARTS):
        part = pl.ds(g * (C // PARTS), C // PARTS)
        loads.append(load(noisy.at[part], buf.at[part], sems.at[g]))
    for copy in small_loads:
        copy.wait()
    taps = []
    for i in range(3):
        taps += [conv_in[i, j] for j in range(3)] + [cond_tap(conv_cond[i, j]) for j in range(3)]
    wts[:, 0:TAPS] = pair_weights(taps)
    wts[:, TAPS:] = pair_weights([conv_out[i, j] for i in range(3) for j in range(3)])
    bias[:, 0:LT] = jnp.broadcast_to(bias_column(bias_in[...]), (2 * C, LT))
    bias[:, LT:] = jnp.broadcast_to(bias_column(bias_out[...]), (2 * C, LT))
    stores = [load(wts, wts_hbm, sems.at[PARTS]), load(bias, bias_hbm, sems.at[PARTS + 1])]
    for copy in loads:
        copy.wait()
    xs[...] = jnp.swapaxes(buf[...], 0, 1).reshape(R * C, W)
    for i, (out, r0) in enumerate(zip((first, second), near_rows())):
        rows = pl.ds(pl.multiple_of(r0 * C, C), 2 * C)
        stores.append(load(xs.at[rows], out, sems.at[PARTS + 2 + i]))
    for copy in stores:
        copy.wait()


def turned(noisy, *small):
    count = len(small)

    def kernel(noisy_ref, *refs):
        scratch = refs[count + 5 :]
        turn_kernel(
            noisy_ref, refs[:count], *refs[count : count + 5], *scratch[:3], scratch[3 : 3 + count], *scratch[3 + count :]
        )

    return pl.pallas_call(
        kernel,
        out_shape=(
            kept((R * C, W)),
            pltpu.HBM((2 * C, W), BF),
            pltpu.HBM((2 * C, W), BF),
            pltpu.HBM((2 * C, TAPS + TAPS_OUT), BF),
            pltpu.HBM((2 * C, 2 * LT), F32),
        ),
        in_specs=hbm(1 + count),
        out_specs=tuple(vmem(1) + hbm(4)),
        scratch_shapes=[
            pltpu.VMEM((C, R, W), BF),
            pltpu.VMEM((2 * C, TAPS + TAPS_OUT), BF),
            pltpu.VMEM((2 * C, 2 * LT), F32),
        ]
        + [pltpu.VMEM(a.shape, a.dtype) for a in small]
        + [pltpu.SemaphoreType.DMA((PARTS + 4,)), pltpu.SemaphoreType.DMA((count,))],
        compiler_params=params(10),
        cost_estimate=pl.CostEstimate(flops=3 * 10**9, bytes_accessed=12 * 10**6, transcendentals=0),
    )(*in_hbm(noisy, *small))


def cond_kernel(got, table_hbm, wts_hbm, bias_hbm, cond, halo, first, second, wts, bias, acc, grp, ints, lists, table, sem, sems):
    me = lax.axis_index("lon")
    left = lax.rem(me + PEERS - 1, PEERS)
    right = lax.rem(me + 1, PEERS)
    for d, p in enumerate((me, left, right)):
        ints[d] = got[p, CP - 16 : CP, :].astype(F32).astype(jnp.int32)
    copy = load(ints, lists, sem)
    loads = []
    for r in range(R // SUBS):
        loads.append(load(table_hbm.at[:, pl.ds(r * W, W)], table.at[r], sems.at[r]))
    others = [load(wts_hbm, wts, sems.at[R // SUBS]), load(bias_hbm, bias, sems.at[R // SUBS + 1])]
    acc[...] = jnp.zeros_like(acc)

    rows = []
    for g in range(C // EDGE):
        cols = slice(g * 32, g * 32 + 32)
        side = [got[p, HELD * CP :, cols].astype(F32) for p in (right, left)]
        rows.append(jnp.concatenate(side + [jnp.zeros((EDGE, 64), F32)], axis=1))
    both = jnp.concatenate(rows, axis=0).astype(BF)
    src = iota((LT, R * LT), 0)
    dst = iota((LT, R * LT), 1)
    at = dst % LT
    kind = jnp.where(at < 64, at, at - 124)
    wanted = ((at < 2) | (at >= 126)) & (src == kind * R + dst // LT)
    place = jnp.where(wanted, 1.0, 0.0).astype(BF)
    tiles = jnp.dot(both, place, preferred_element_type=F32).astype(BF)
    for r in range(R):
        halo[pl.ds(r * C, C), :] = tiles[:, r * LT : (r + 1) * LT]

    copy.wait()
    for d in range(3):
        for s in range(SUBS):
            for k in range(SLOTS):
                n = s * SLOTS + k
                block = lists[d, 14, n]
                part = got[block // HELD, pl.ds(pl.multiple_of(lax.rem(block, HELD) * CP, CP), CP), :]
                at = (d * SUBS + s) * (KINDS + 1) + lists[d, 14, 16 + n]
                acc[at] = acc[at] + part.astype(F32)
    for d in range(3):
        for s in range(SUBS):
            for w in range(KINDS):
                grp[d, pl.ds(s * CP, CP), w * LT : (w + 1) * LT] = acc[(d * SUBS + s) * (KINDS + 1) + w].astype(BF)

    lane = iota((SUBS * CP, LT), 1)
    for r in range(R // SUBS):
        if r % 2 == 0:
            loads[r].wait()
            loads[r + 1].wait()
            lt = jnp.concatenate([table[q, :, W - LT : W] for q in (r, r + 1)], axis=1)
            rt = jnp.concatenate([table[q, :, 0:LT] for q in (r, r + 1)], axis=1)
            lhs_2 = jnp.dot(grp[1], lt, preferred_element_type=F32)
            rhs_2 = jnp.dot(grp[2], rt, preferred_element_type=F32)
        part = table.at[r]
        tile = slice(r % 2 * LT, (r % 2 + 1) * LT)
        own = jnp.dot(grp[0], part[...], preferred_element_type=F32).astype(BF)
        lhs, rhs = lhs_2[:, tile], rhs_2[:, tile]
        side = jnp.where(lane < 2, rhs, jnp.where(lane >= 126, lhs, 0.0)).astype(BF)
        for s in range(SUBS):
            at = pl.ds((s * SUBS + r) * CP, CP)
            cond[at, 0:W] = own[s * CP : (s + 1) * CP]
            cond[at, W:WX] = side[s * CP : (s + 1) * CP]
    for out, r0 in zip((first, second), near_rows()):
        out[:, 0:WX] = cond[pl.ds(pl.multiple_of(r0 * CP, CP), 2 * CP), :]
        for j in range(2):
            out[:, WX + j * LT : WX + (j + 1) * LT] = halo[pl.ds(pl.multiple_of((r0 + j) * C, C), C), :]
    for copy in others:
        copy.wait()


def cond_tile(got, table, wts, bias):
    edge = struct((2 * CP, WX + 2 * LT))
    return pl.pallas_call(
        cond_kernel,
        out_shape=(
            kept((R * CP, WX)),
            kept((R * C, LT)),
            edge,
            edge,
            kept(wts.shape),
            kept(bias.shape, F32),
        ),
        in_specs=vmem(1) + hbm(3),
        out_specs=tuple(vmem(6)),
        scratch_shapes=[
            pltpu.VMEM((3 * SUBS * (KINDS + 1), CP, LT), F32),
            pltpu.VMEM((3, SUBS * CP, KINDS * LT), BF),
            pltpu.VMEM((3, 16, LT), jnp.int32),
            pltpu.SMEM((3, 16, LT), jnp.int32),
            pltpu.VMEM((R // SUBS, KINDS * LT, W), BF),
            pltpu.SemaphoreType.DMA,
            pltpu.SemaphoreType.DMA((R // SUBS + 2,)),
        ],
        compiler_params=params(14),
    )(*in_vmem(got), *in_hbm(table, wts, bias))


def silu(v):
    return v / (1.0 + jnp.exp(-v))


def put_taps(dst, row, noisy, cond):
    at = row * TAP
    for d, y in enumerate(shifted(noisy, WX)):
        dst[pl.ds(at + d * C, C), :] = y
    for d, y in enumerate(shifted(cond, WX)):
        dst[pl.ds(at + 3 * C + d * CP, CP), :] = y


def put_act(dst, row, x):
    for d, y in enumerate(shifted(x, WX)):
        dst[pl.ds((row * 3 + d) * C, C), :] = y[:, 0:W]


def own_row(xs, halo, r):
    return jnp.concatenate([xs[pl.ds(r * C, C), :], halo[pl.ds(r * C, C), :]], axis=1)


def first_conv(wts, bias, rows):
    return silu(jnp.dot(wts[:, 0:TAPS], rows, preferred_element_type=F32) + bias[:, 0:1])


def second_conv(wts, bias, rows, x):
    y = jnp.dot(wts[:, TAPS:], rows, preferred_element_type=F32)
    return (y + x.astype(F32) + bias[:, LT : LT + 1]).astype(BF)


def inner_kernel(cond, halo, xs, wts, bias, noisy_hbm, zi, edge, noisy_2, x3, a3, sem):
    near = load(noisy_hbm, noisy_2, sem)
    for r in range(R):
        put_taps(x3, r, own_row(xs, halo, r), cond[pl.ds(r * CP, CP), :])
    for i in range(PAIRS):
        a = first_conv(wts, bias, x3[pl.ds(2 * i * TAP, TAPS), :]).astype(BF)
        for j in range(2):
            r = i * 2 + j
            x = a[j * C : (j + 1) * C]
            if r < 2 or r >= R - 4:
                edge[pl.ds((r if r < 2 else r - R + 6) * C, C), :] = x
            put_act(a3, r, x)
    for i in range(PAIRS - 1):
        x = xs[pl.ds((i + 1) * 2 * C, 2 * C), :]
        zi[pl.ds(i * 2 * C, 2 * C), :] = second_conv(wts, bias, a3[pl.ds(i * 6 * C, TAPS_OUT), :], x)
    near.wait()


def inner_rows(cond, halo, xs, wts, bias, noisy_2):
    return pl.pallas_call(
        inner_kernel,
        out_shape=(kept(((R - 4) * C, W)), kept((4 * C, WX)), kept((2 * C, W))),
        in_specs=vmem(5) + hbm(1),
        out_specs=tuple(vmem(3)),
        scratch_shapes=[
            pltpu.VMEM((R * TAP, WX), BF),
            pltpu.VMEM(((R - 2) * 3 * C, W), BF),
            pltpu.SemaphoreType.DMA,
        ],
        compiler_params=params(26),
        cost_estimate=pl.CostEstimate(flops=6 * 10**9, bytes_accessed=12 * 10**6, transcendentals=10**6),
    )(*in_vmem(cond, halo, xs, wts, bias), *in_hbm(noisy_2))


def outer_kernel(
    zi, edge, cond, halo, noisy_1, noisy_2, got_1, got_2, xs, wts, bias, out, x3, a3, buf, sems
):
    lat = lax.axis_index("lat")
    half = R // 2
    each = C // PARTS
    upper = jnp.where(lat == 0, 0.0, 1.0)
    lower = jnp.where(lat == lax.axis_size("lat") - 1, 0.0, 1.0)

    def both_sides(odd):
        copies = []
        sides = ((1 - odd, got_1), (odd, got_2))
        for k, (low, _) in enumerate(sides):
            for j in range(2):
                put_act(a3.at[k], (1 - low) * 2 + j, edge[pl.ds((low * 2 + j) * C, C), :])
                r = low * (R - 2) + j
                put_taps(x3.at[k], (1 - low) * 2 + j, own_row(xs, halo, r), cond[pl.ds(r * CP, CP), :])
        for k, (low, got) in enumerate(sides):
            noisy = noisy_2 if k else noisy_1
            for j in range(2):
                tile = got[:, WX + j * LT : WX + (j + 1) * LT]
                x = jnp.concatenate([noisy[pl.ds(j * C, C), :], tile], axis=1)
                put_taps(x3.at[k], low * 2 + j, x, got[j * CP : (j + 1) * CP, 0:WX])
            v = first_conv(wts, bias, x3[k])
            v0, v1 = (v[0:C], v[C:] * lower) if low else (v[0:C] * upper, v[C:])
            put_act(a3.at[k], low * 2, v0.astype(BF))
            put_act(a3.at[k], low * 2 + 1, v1.astype(BF))
            z = second_conv(wts, bias, a3[k], xs[pl.ds(low * (R - 2) * C, 2 * C), :])
            rows = [z[0:C], z[C:]]
            inner = [zi[pl.ds((low * (half - 2) + r) * C, C), :] for r in range(half - 2)]
            rows = inner + rows if low else rows + inner
            here = pl.ds(low * half, half)
            for g in range(PARTS):
                chans = pl.ds(g * each, each)
                group = jnp.stack([row[g * each : (g + 1) * each] for row in rows], axis=0)
                buf[k, chans] = jnp.swapaxes(group, 0, 1)
                copies.append(load(buf.at[k, chans], out.at[chans, here, :], sems.at[k * PARTS + g]))
        for copy in copies:
            copy.wait()

    for odd in range(2):
        pl.when(lax.rem(lat, 2) == odd)(lambda odd=odd: both_sides(odd))


def outer_rows(zi, edge, cond, halo, noisy_1, noisy_2, got_1, got_2, xs, wts, bias):
    return pl.pallas_call(
        outer_kernel,
        out_shape=pltpu.HBM((C, R, W), BF),
        in_specs=vmem(11),
        out_specs=hbm(1)[0],
        scratch_shapes=[
            pltpu.VMEM((2, TAPS, WX), BF),
            pltpu.VMEM((2, TAPS_OUT, W), BF),
            pltpu.VMEM((2, C, R // 2, W), BF),
            pltpu.SemaphoreType.DMA((2 * PARTS,)),
        ],
        compiler_params=params(24),
    )(*in_vmem(zi, edge, cond, halo), noisy_1, *in_vmem(noisy_2), got_1, got_2, *in_vmem(xs, wts, bias))


def exchanged(first, second):
    count = lax.axis_size("lat")
    got_1 = lax.ppermute(first, "lat", [(i, i ^ 1) for i in range(count)])
    got_2 = lax.ppermute(second, "lat", [(i, ((i + 1) ^ 1) - 1) for i in range(1, count - 1)])
    return got_1, got_2


def local(noisy, coarse, owner, slot, weight, counts, table, conv_in, conv_cond, bias_in, conv_out, bias_out):
    coarse = jnp.transpose(coarse, (0, 2, 1, 3))
    conv_cond = jnp.transpose(conv_cond, (0, 1, 3, 2))
    table = table.reshape(KINDS * LT, table.shape[2])
    msg = message(noisy, coarse, owner, slot, weight, counts)
    got = lax.all_to_all(msg, "lon", split_axis=0, concat_axis=0, tiled=True)
    xs, first, second, wts, bias = turned(noisy, conv_in, conv_cond, conv_out, bias_in[None], bias_out[None])
    noisy_1, noisy_2 = exchanged(first, second)
    cond, halo, first, second, wts, bias = cond_tile(got, table, wts, bias)
    got_1, got_2 = exchanged(first, second)
    zi, edge, noisy_2 = inner_rows(cond, halo, xs, wts, bias, noisy_2)
    return outer_rows(zi, edge, cond, halo, noisy_1, noisy_2, got_1, got_2, xs, wts, bias)


def solution(mesh):
    grid = P("lat", "lon")
    in_specs = (P(None, "lat", "lon"),) + (grid,) * 5 + (P(),) * 6
    return jax.shard_map(local, mesh=mesh, in_specs=in_specs, out_specs=P(None, "lat", "lon"), check_vma=False)
```

```python
import jax
import jax.numpy as jnp
from jax import lax
from jax.experimental import pallas as pl
from jax.experimental.pallas import tpu as pltpu
from jax.sharding import PartitionSpec as P

BF = jnp.bfloat16
F32 = jnp.float32
MIB = 1024 * 1024

C = 64
CP = 32
R = 16
W = 1280
LT = 128
WX = W + LT
PEERS = 16
HELD = 4
SUBS = 4
SLOTS = 4
KINDS = 4
EDGE = 16
MSG = HELD * CP + EDGE
PAIRS = R // 2 - 1
TAP = 3 * (C + CP)
TAPS = 4 * TAP
TAPS_OUT = 12 * C
PARTS = 4


def vmem(n=1):
    return [pl.BlockSpec(memory_space=pltpu.VMEM)] * n


def smem(n=1):
    return [pl.BlockSpec(memory_space=pltpu.SMEM)] * n


def params(mib):
    return pltpu.CompilerParams(vmem_limit_bytes=mib * MIB)


def struct(shape, dtype=BF):
    return jax.ShapeDtypeStruct(shape, dtype)


def kept(shape, dtype=BF):
    return pltpu.VMEM(shape, dtype)


def hbm(n=1):
    return [pl.BlockSpec(memory_space=pltpu.HBM)] * n


def in_hbm(*arrays):
    return [pltpu.with_memory_space_constraint(a, pltpu.HBM) for a in arrays]


def in_vmem(*arrays):
    return [pltpu.with_memory_space_constraint(a, pltpu.VMEM) for a in arrays]


def iota(shape, dim):
    return lax.broadcasted_iota(jnp.int32, shape, dim)


def message_kernel(noisy, coarse_hbm, ids, out, tiles, coarse, owner, slot, weight, counts, sems):
    me = lax.axis_index("lon")
    loads = [
        load(noisy.at[:, :, 0:LT], tiles.at[0], sems.at[0]),
        load(noisy.at[:, :, W - LT : W], tiles.at[1], sems.at[1]),
        load(coarse_hbm, coarse, sems.at[2]),
    ]
    loads += [load(a, b, sems.at[3 + i]) for i, (a, b) in enumerate(zip(ids, (owner, slot, weight, counts)))]
    for copy in loads:
        copy.wait()
    lane = iota((C, R, LT), 2)
    edge = jnp.where(lane < 64, tiles[0].astype(F32), tiles[1].astype(F32))
    edge = jnp.swapaxes(edge.astype(BF), 0, 1)
    edge = jnp.concatenate([edge[r] for r in range(R)], axis=1)
    row = iota((R * LT, LT), 0)
    col = iota((R * LT, LT), 1)
    at = row % LT
    kind = jnp.where(at < 64, at, at - 124)
    wanted = ((at < 2) | (at >= 126)) & (col == kind * R + row // LT)
    pick = jnp.where(wanted, 1.0, 0.0).astype(BF)
    packed = jnp.dot(edge, pick, preferred_element_type=F32)
    sides = []
    for side in range(2):
        parts = [packed[g * EDGE : (g + 1) * EDGE, side * 32 : side * 32 + 32] for g in range(C // EDGE)]
        sides.append(jnp.concatenate(parts, axis=1))
    lanes = iota((2, HELD, LT), 2)
    lists = jnp.zeros((2, HELD, LT), F32)
    for s in range(SUBS):
        live = counts[0, 0, s]
        for k in range(SLOTS):
            n = s * SLOTS + k
            block = owner[0, 0, s, k] * HELD + slot[0, 0, s, k]
            kind_id = jnp.where(k < live, weight[0, 0, s, k], KINDS)
            lists = jnp.where(lanes == n, block.astype(F32), lists)
            lists = jnp.where(lanes == 16 + n, kind_id.astype(F32), lists)
    chans = coarse[0].astype(F32)
    blocks = jnp.swapaxes(jnp.concatenate([chans, lists], axis=0), 0, 1)
    blocks = blocks.reshape(HELD * CP, LT).astype(BF)
    right = lax.rem(me + 1, PEERS)
    for p in range(PEERS):
        out[p, 0 : HELD * CP] = blocks
        out[p, HELD * CP :] = jnp.where(right == p, sides[1], sides[0]).astype(BF)


def message(noisy, coarse, *ids):
    def kernel(noisy_ref, coarse_ref, owner, slot, weight, counts, *rest):
        message_kernel(noisy_ref, coarse_ref, (owner, slot, weight, counts), *rest)

    return pl.pallas_call(
        kernel,
        out_shape=kept((PEERS, MSG, LT)),
        in_specs=hbm(6),
        out_specs=vmem()[0],
        scratch_shapes=[pltpu.VMEM((2, C, R, LT), BF), pltpu.VMEM(coarse.shape, BF)]
        + [pltpu.SMEM(a.shape, jnp.int32) for a in ids]
        + [pltpu.SemaphoreType.DMA((7,))],
        compiler_params=params(12),
    )(*in_hbm(noisy, coarse, *ids))


def load(src, dst, sem):
    copy = pltpu.make_async_copy(src, dst, sem)
    copy.start()
    return copy


def shifted(x, width):
    return [pltpu.roll(x, 1, 1), x, pltpu.roll(x, width - 1, 1)]


def pair_weights(taps):
    rows = jnp.concatenate(taps, axis=1)
    blank = jnp.zeros((rows.shape[0], rows.shape[1] // 3), BF)
    return jnp.concatenate(
        [jnp.concatenate([rows, blank], axis=1), jnp.concatenate([blank, rows], axis=1)], axis=0
    )


def cond_tap(tap):
    tap = jnp.concatenate([tap.astype(F32), jnp.zeros((CP - tap.shape[0], tap.shape[1]), F32)], axis=0)
    return tap.T.astype(BF)


def bias_column(row):
    same = iota((C, C), 0) == iota((C, C), 1)
    column = jnp.sum(jnp.where(same, row, 0.0), axis=1, keepdims=True)
    return jnp.concatenate([column, column], axis=0)


def near_rows():
    odd = lax.rem(lax.axis_index("lat"), 2)
    return (1 - odd) * (R - 2), odd * (R - 2)


def turn_kernel(
    noisy, params_hbm, xs, first, second, wts_hbm, bias_hbm, buf, wts, bias, small, sems, small_sems
):
    small_loads = [load(a, b, small_sems.at[i]) for i, (a, b) in enumerate(zip(params_hbm, small))]
    conv_in, conv_cond, conv_out, bias_in, bias_out = small
    loads = []
    for g in range(PARTS):
        part = pl.ds(g * (C // PARTS), C // PARTS)
        loads.append(load(noisy.at[part], buf.at[part], sems.at[g]))
    for copy in small_loads:
        copy.wait()
    taps = []
    for i in range(3):
        taps += [conv_in[i, j] for j in range(3)] + [cond_tap(conv_cond[i, j]) for j in range(3)]
    wts[:, 0:TAPS] = pair_weights(taps)
    wts[:, TAPS:] = pair_weights([conv_out[i, j] for i in range(3) for j in range(3)])
    bias[:, 0:LT] = jnp.broadcast_to(bias_column(bias_in[...]), (2 * C, LT))
    bias[:, LT:] = jnp.broadcast_to(bias_column(bias_out[...]), (2 * C, LT))
    stores = [load(wts, wts_hbm, sems.at[PARTS]), load(bias, bias_hbm, sems.at[PARTS + 1])]
    for copy in loads:
        copy.wait()
    xs[...] = jnp.swapaxes(buf[...], 0, 1).reshape(R * C, W)
    for i, (out, r0) in enumerate(zip((first, second), near_rows())):
        rows = pl.ds(pl.multiple_of(r0 * C, C), 2 * C)
        stores.append(load(xs.at[rows], out, sems.at[PARTS + 2 + i]))
    for copy in stores:
        copy.wait()


def turned(noisy, *small):
    count = len(small)

    def kernel(noisy_ref, *refs):
        scratch = refs[count + 5 :]
        turn_kernel(
            noisy_ref, refs[:count], *refs[count : count + 5], *scratch[:3], scratch[3 : 3 + count], *scratch[3 + count :]
        )

    return pl.pallas_call(
        kernel,
        out_shape=(
            kept((R * C, W)),
            pltpu.HBM((2 * C, W), BF),
            pltpu.HBM((2 * C, W), BF),
            pltpu.HBM((2 * C, TAPS + TAPS_OUT), BF),
            pltpu.HBM((2 * C, 2 * LT), F32),
        ),
        in_specs=hbm(1 + count),
        out_specs=tuple(vmem(1) + hbm(4)),
        scratch_shapes=[
            pltpu.VMEM((C, R, W), BF),
            pltpu.VMEM((2 * C, TAPS + TAPS_OUT), BF),
            pltpu.VMEM((2 * C, 2 * LT), F32),
        ]
        + [pltpu.VMEM(a.shape, a.dtype) for a in small]
        + [pltpu.SemaphoreType.DMA((PARTS + 4,)), pltpu.SemaphoreType.DMA((count,))],
        compiler_params=params(10),
        cost_estimate=pl.CostEstimate(flops=3 * 10**9, bytes_accessed=12 * 10**6, transcendentals=0),
    )(*in_hbm(noisy, *small))


def cond_kernel(got, table_hbm, wts_hbm, bias_hbm, cond, halo, first, second, wts, bias, acc, grp, ints, lists, table, sem, sems):
    me = lax.axis_index("lon")
    left = lax.rem(me + PEERS - 1, PEERS)
    right = lax.rem(me + 1, PEERS)
    for d, p in enumerate((me, left, right)):
        ints[d] = got[p, CP - 16 : CP, :].astype(F32).astype(jnp.int32)
    copy = load(ints, lists, sem)
    loads = []
    for r in range(R // SUBS):
        loads.append(load(table_hbm.at[:, pl.ds(r * W, W)], table.at[r], sems.at[r]))
    others = [load(wts_hbm, wts, sems.at[R // SUBS]), load(bias_hbm, bias, sems.at[R // SUBS + 1])]
    acc[...] = jnp.zeros_like(acc)

    rows = []
    for g in range(C // EDGE):
        cols = slice(g * 32, g * 32 + 32)
        side = [got[p, HELD * CP :, cols].astype(F32) for p in (right, left)]
        rows.append(jnp.concatenate(side + [jnp.zeros((EDGE, 64), F32)], axis=1))
    both = jnp.concatenate(rows, axis=0).astype(BF)
    src = iota((LT, R * LT), 0)
    dst = iota((LT, R * LT), 1)
    at = dst % LT
    kind = jnp.where(at < 64, at, at - 124)
    wanted = ((at < 2) | (at >= 126)) & (src == kind * R + dst // LT)
    place = jnp.where(wanted, 1.0, 0.0).astype(BF)
    tiles = jnp.dot(both, place, preferred_element_type=F32).astype(BF)
    for r in range(R):
        halo[pl.ds(r * C, C), :] = tiles[:, r * LT : (r + 1) * LT]

    copy.wait()
    for d in range(3):
        for s in range(SUBS):
            for k in range(SLOTS):
                n = s * SLOTS + k
                block = lists[d, 14, n]
                part = got[block // HELD, pl.ds(pl.multiple_of(lax.rem(block, HELD) * CP, CP), CP), :]
                at = (d * SUBS + s) * (KINDS + 1) + lists[d, 14, 16 + n]
                acc[at] = acc[at] + part.astype(F32)
    for d in range(3):
        for s in range(SUBS):
            for w in range(KINDS):
                grp[d, pl.ds(s * CP, CP), w * LT : (w + 1) * LT] = acc[(d * SUBS + s) * (KINDS + 1) + w].astype(BF)

    lane = iota((SUBS * CP, LT), 1)
    for r in range(R // SUBS):
        loads[r].wait()
        own = jnp.dot(grp[0], table[r], preferred_element_type=F32).astype(BF)
        for s in range(SUBS):
            cond[pl.ds((s * SUBS + r) * CP, CP), 0:W] = own[s * CP : (s + 1) * CP]
        if r % 2 == 1:
            lt = jnp.concatenate([table[q, :, W - LT : W] for q in (r - 1, r)], axis=1)
            rt = jnp.concatenate([table[q, :, 0:LT] for q in (r - 1, r)], axis=1)
            lhs = jnp.dot(grp[1], lt, preferred_element_type=F32)
            rhs = jnp.dot(grp[2], rt, preferred_element_type=F32)
            for j in range(2):
                tile = slice(j * LT, (j + 1) * LT)
                side = jnp.where(lane < 2, rhs[:, tile], jnp.where(lane >= 126, lhs[:, tile], 0.0)).astype(BF)
                for s in range(SUBS):
                    cond[pl.ds((s * SUBS + r - 1 + j) * CP, CP), W:WX] = side[s * CP : (s + 1) * CP]
    for out, r0 in zip((first, second), near_rows()):
        out[:, 0:WX] = cond[pl.ds(pl.multiple_of(r0 * CP, CP), 2 * CP), :]
        for j in range(2):
            out[:, WX + j * LT : WX + (j + 1) * LT] = halo[pl.ds(pl.multiple_of((r0 + j) * C, C), C), :]
    for copy in others:
        copy.wait()


def cond_tile(got, table, wts, bias):
    edge = struct((2 * CP, WX + 2 * LT))
    return pl.pallas_call(
        cond_kernel,
        out_shape=(
            kept((R * CP, WX)),
            kept((R * C, LT)),
            edge,
            edge,
            kept(wts.shape),
            kept(bias.shape, F32),
        ),
        in_specs=vmem(1) + hbm(3),
        out_specs=tuple(vmem(6)),
        scratch_shapes=[
            pltpu.VMEM((3 * SUBS * (KINDS + 1), CP, LT), F32),
            pltpu.VMEM((3, SUBS * CP, KINDS * LT), BF),
            pltpu.VMEM((3, 16, LT), jnp.int32),
            pltpu.SMEM((3, 16, LT), jnp.int32),
            pltpu.VMEM((R // SUBS, KINDS * LT, W), BF),
            pltpu.SemaphoreType.DMA,
            pltpu.SemaphoreType.DMA((R // SUBS + 2,)),
        ],
        compiler_params=params(14),
    )(*in_vmem(got), *in_hbm(table, wts, bias))


def silu(v):
    return v / (1.0 + jnp.exp(-v))


def put_taps(dst, row, noisy, cond):
    at = row * TAP
    for d, y in enumerate(shifted(noisy, WX)):
        dst[pl.ds(at + d * C, C), :] = y
    for d, y in enumerate(shifted(cond, WX)):
        dst[pl.ds(at + 3 * C + d * CP, CP), :] = y


def put_act(dst, row, x):
    for d, y in enumerate(shifted(x, WX)):
        dst[pl.ds((row * 3 + d) * C, C), :] = y[:, 0:W]


def own_row(xs, halo, r):
    return jnp.concatenate([xs[pl.ds(r * C, C), :], halo[pl.ds(r * C, C), :]], axis=1)


def first_conv(wts, bias, rows):
    return silu(jnp.dot(wts[:, 0:TAPS], rows, preferred_element_type=F32) + bias[:, 0:1])


def second_conv(wts, bias, rows, x):
    y = jnp.dot(wts[:, TAPS:], rows, preferred_element_type=F32)
    return (y + x.astype(F32) + bias[:, LT : LT + 1]).astype(BF)


def inner_kernel(cond, halo, xs, wts, bias, noisy_hbm, zi, edge, noisy_2, x3, a3, sem):
    near = load(noisy_hbm, noisy_2, sem)
    for r in range(R):
        put_taps(x3, r, own_row(xs, halo, r), cond[pl.ds(r * CP, CP), :])
    for i in range(PAIRS):
        a = first_conv(wts, bias, x3[pl.ds(2 * i * TAP, TAPS), :]).astype(BF)
        for j in range(2):
            r = i * 2 + j
            x = a[j * C : (j + 1) * C]
            if r < 2 or r >= R - 4:
                edge[pl.ds((r if r < 2 else r - R + 6) * C, C), :] = x
            put_act(a3, r, x)
    for i in range(PAIRS - 1):
        x = xs[pl.ds((i + 1) * 2 * C, 2 * C), :]
        zi[pl.ds(i * 2 * C, 2 * C), :] = second_conv(wts, bias, a3[pl.ds(i * 6 * C, TAPS_OUT), :], x)
    near.wait()


def inner_rows(cond, halo, xs, wts, bias, noisy_2):
    return pl.pallas_call(
        inner_kernel,
        out_shape=(kept(((R - 4) * C, W)), kept((4 * C, WX)), kept((2 * C, W))),
        in_specs=vmem(5) + hbm(1),
        out_specs=tuple(vmem(3)),
        scratch_shapes=[
            pltpu.VMEM((R * TAP, WX), BF),
            pltpu.VMEM(((R - 2) * 3 * C, W), BF),
            pltpu.SemaphoreType.DMA,
        ],
        compiler_params=params(26),
        cost_estimate=pl.CostEstimate(flops=6 * 10**9, bytes_accessed=12 * 10**6, transcendentals=10**6),
    )(*in_vmem(cond, halo, xs, wts, bias), *in_hbm(noisy_2))


def outer_kernel(
    zi, edge, cond, halo, noisy_1, noisy_2, got_1, got_2, xs, wts, bias, out, x3, a3, buf, sems
):
    lat = lax.axis_index("lat")
    half = R // 2
    each = C // PARTS
    upper = jnp.where(lat == 0, 0.0, 1.0)
    lower = jnp.where(lat == lax.axis_size("lat") - 1, 0.0, 1.0)

    def both_sides(odd):
        copies = []
        sides = ((1 - odd, got_1), (odd, got_2))
        for k, (low, _) in enumerate(sides):
            for j in range(2):
                put_act(a3.at[k], (1 - low) * 2 + j, edge[pl.ds((low * 2 + j) * C, C), :])
                r = low * (R - 2) + j
                put_taps(x3.at[k], (1 - low) * 2 + j, own_row(xs, halo, r), cond[pl.ds(r * CP, CP), :])
        for k, (low, got) in enumerate(sides):
            noisy = noisy_2 if k else noisy_1
            for j in range(2):
                tile = got[:, WX + j * LT : WX + (j + 1) * LT]
                x = jnp.concatenate([noisy[pl.ds(j * C, C), :], tile], axis=1)
                put_taps(x3.at[k], low * 2 + j, x, got[j * CP : (j + 1) * CP, 0:WX])
            v = first_conv(wts, bias, x3[k])
            v0, v1 = (v[0:C], v[C:] * lower) if low else (v[0:C] * upper, v[C:])
            put_act(a3.at[k], low * 2, v0.astype(BF))
            put_act(a3.at[k], low * 2 + 1, v1.astype(BF))
            z = second_conv(wts, bias, a3[k], xs[pl.ds(low * (R - 2) * C, 2 * C), :])
            rows = [z[0:C], z[C:]]
            inner = [zi[pl.ds((low * (half - 2) + r) * C, C), :] for r in range(half - 2)]
            rows = inner + rows if low else rows + inner
            here = pl.ds(low * half, half)
            for g in range(PARTS):
                chans = pl.ds(g * each, each)
                group = jnp.stack([row[g * each : (g + 1) * each] for row in rows], axis=0)
                buf[k, chans] = jnp.swapaxes(group, 0, 1)
                copies.append(load(buf.at[k, chans], out.at[chans, here, :], sems.at[k * PARTS + g]))
        for copy in copies:
            copy.wait()

    for odd in range(2):
        pl.when(lax.rem(lat, 2) == odd)(lambda odd=odd: both_sides(odd))


def outer_rows(zi, edge, cond, halo, noisy_1, noisy_2, got_1, got_2, xs, wts, bias):
    return pl.pallas_call(
        outer_kernel,
        out_shape=pltpu.HBM((C, R, W), BF),
        in_specs=vmem(11),
        out_specs=hbm(1)[0],
        scratch_shapes=[
            pltpu.VMEM((2, TAPS, WX), BF),
            pltpu.VMEM((2, TAPS_OUT, W), BF),
            pltpu.VMEM((2, C, R // 2, W), BF),
            pltpu.SemaphoreType.DMA((2 * PARTS,)),
        ],
        compiler_params=params(24),
    )(*in_vmem(zi, edge, cond, halo), noisy_1, *in_vmem(noisy_2), got_1, got_2, *in_vmem(xs, wts, bias))


def exchanged(first, second):
    count = lax.axis_size("lat")
    got_1 = lax.ppermute(first, "lat", [(i, i ^ 1) for i in range(count)])
    got_2 = lax.ppermute(second, "lat", [(i, ((i + 1) ^ 1) - 1) for i in range(1, count - 1)])
    return got_1, got_2


def local(noisy, coarse, owner, slot, weight, counts, table, conv_in, conv_cond, bias_in, conv_out, bias_out):
    coarse = jnp.transpose(coarse, (0, 2, 1, 3))
    conv_cond = jnp.transpose(conv_cond, (0, 1, 3, 2))
    table = table.reshape(KINDS * LT, table.shape[2])
    msg = message(noisy, coarse, owner, slot, weight, counts)
    got = lax.all_to_all(msg, "lon", split_axis=0, concat_axis=0, tiled=True)
    xs, first, second, wts, bias = turned(noisy, conv_in, conv_cond, conv_out, bias_in[None], bias_out[None])
    noisy_1, noisy_2 = exchanged(first, second)
    cond, halo, first, second, wts, bias = cond_tile(got, table, wts, bias)
    got_1, got_2 = exchanged(first, second)
    zi, edge, noisy_2 = inner_rows(cond, halo, xs, wts, bias, noisy_2)
    return outer_rows(zi, edge, cond, halo, noisy_1, noisy_2, got_1, got_2, xs, wts, bias)


def solution(mesh):
    grid = P("lat", "lon")
    in_specs = (P(None, "lat", "lon"),) + (grid,) * 5 + (P(),) * 6
    return jax.shard_map(local, mesh=mesh, in_specs=in_specs, out_specs=P(None, "lat", "lon"), check_vma=False)
```
